128 devices in a mesh: req: 8 (over y, core), exp: 16 (over x, z).
Axes of the slice: x: 4, y: 4, z: 4, core: 2. Of those that a mesh axis runs over, the one named last changes fastest.
Arguments:
- residual: bfloat16 [8320, 2048], P(('req', 'exp')), may hold values from -6 to 6
- prefill_qkv: bfloat16 [16, 3, 512, 2048], P('req', None, None, 'exp'), may hold values from -4.5 to 4.5
- decode_qkv: bfloat16 [128, 3, 2048], P('req', None, 'exp'), may hold values from -4.5 to 4.5
- cache_pool: bfloat16 [2, 992, 128, 2048], P(None, 'req', None, 'exp'), may hold values from -4.5 to 4.5
- page_table: int32 [128, 64], P('req'), may hold values from 0 to 123, as said below
- cache_len: int32 [128], P('req'), may hold values from 2 to 8192
- out_weight: bfloat16 [2048, 2048], P('exp'), may hold values from -0.125 to 0.125
- norm_gain: float32 [2048], replicated, may hold values from 0.1 to 1.9
- shared_gate_up: bfloat16 [2, 2048, 5632], P(None, None, 'exp'), may hold values from -0.125 to 0.125
- shared_down: bfloat16 [5632, 2048], P('exp'), may hold values from -0.078125 to 0.078125
- shared_gate: bfloat16 [2048], replicated, may hold values from -0.25 to 0.25
- routes: int32 [8320, 4], P(('req', 'exp')), may hold values from 0 to 63, all different within a row; in each aligned block of 65 rows (0 to 64, 65 to 129, ...) at most 8 rows name the same one
- route_weight: float32 [8320, 4], P(('req', 'exp')), may hold values from 0.1 to 0.5
- expert_gate_up: bfloat16 [128, 2, 2048, 704], P(('req', 'exp')), may hold values from -0.125 to 0.125
- expert_down: bfloat16 [128, 704, 2048], P(('req', 'exp')), may hold values from -0.15625 to 0.15625
Outputs:
- layer_out: bfloat16 [8320, 2048], P(('req', 'exp'))
The draws below stay inside these ranges and needn't reach their ends.
Inputs may be any that keep to these rules, and one draw needn't show every extreme that they name: `page_table`: for decode request i the first ceil(cache_len[i] / 128) entries name distinct pages among the requests of one req index and hold its cache in order; later entries name pages but are not read. `routes`: in the rows of one device (aligned blocks of 65 rows) no expert is named more than 8 times; a row names 4 different experts.
All inputs are finite; a program needn't handle non-finite values.
Results may differ from the reference program's by a relative error of at most 0.015.
Values may be sent and summed in bfloat16 or wider, within the bound.
No kernel may reach another device: no remote copies, remote signals or barrier semaphores. Data moves between devices by JAX's collectives and lax.ppermute only.
A program may use at most 128 MiB of HBM per device.

```python
import math
import jax
import jax.numpy as jnp
import numpy as np
from jax import lax

D = 2048
HEADS = 16
HD = 128
FE = 1408
FS = 5632
TOPK = 4
SPAN = 512
PRE_DEV = 2
DEC_DEV = 16
PAGE = 128
MAXLEN = 8192
EXPERTS = 64
SPLIT = 2
FE_DEV = 704
FS_DEV = 352
MAXPAGES = 64
SHORTPAGES = 4
PAGES_DEV = 124
T_DEV = 65
CAP = 8
PREFILL = 16
DECODE = 128
PAGES = 992
TOKENS = 8320
SHARDS = 128
N_REQ = 8
N_EXP = 16
DEVICES = 128


def shuffle_pages(page_key):
    return jax.random.permutation(page_key, PAGES_DEV)


def pick_pages(shuffled_row, slot_rows):
    return shuffled_row[slot_rows]


def pages_and_lengths(key):
    base_key = jax.random.fold_in(key, 7)
    first_key, second_key, third_key = jax.random.split(base_key, 3)
    long_slot = jax.random.randint(first_key, (N_REQ, 1), 0, DEC_DEV)
    short_len = jax.random.randint(second_key, (N_REQ, DEC_DEV), 2, SHORTPAGES * PAGE + 1)
    request_order = jnp.arange(DEC_DEV)[None, :]
    lengths = jnp.where(request_order == long_slot, MAXLEN, short_len)
    shuffled = jax.vmap(shuffle_pages)(jax.random.split(third_key, N_REQ))
    first_page = request_order * SHORTPAGES + (MAXPAGES - SHORTPAGES) * (request_order > long_slot).astype(jnp.int32)
    page_slots = (first_page[:, :, None] + jnp.arange(MAXPAGES)[None, None, :]) % PAGES_DEV
    page_rows = jax.vmap(pick_pages)(shuffled, page_slots)
    return (page_rows.reshape(DECODE, MAXPAGES).astype(jnp.int32), lengths.reshape(DECODE).astype(jnp.int32))


def base_values(key, shape):
    return jnp.clip(jax.random.normal(key, shape, jnp.float32), -4.0, 4.0)


def draw_prefill_qkv(key, part):
    values = base_values(jax.random.fold_in(key, 1), (PREFILL, 3, SPAN, D))
    return values.astype(jnp.bfloat16)


def draw_decode_qkv(key, part):
    values = base_values(jax.random.fold_in(key, 2), (DECODE, 3, D))
    return values.astype(jnp.bfloat16)


def draw_cache_pool(key, part):
    values = base_values(jax.random.fold_in(key, 4), (2, PAGES, PAGE, D))
    return values.astype(jnp.bfloat16)


def draw_page_table(key, part):
    return pages_and_lengths(key)[0]


def draw_cache_len(key, part):
    return pages_and_lengths(key)[1]


def steps_of(rng, dims, cuts, smallest, largest):
    loudness = 1.0
    for dim, parts in cuts:
        draws = jax.random.uniform(jax.random.fold_in(jax.random.fold_in(rng, 6), dim), (parts,), jnp.float32, smallest / len(cuts), largest / len(cuts))
        loudness = loudness * jnp.repeat(jnp.exp(draws), dims[dim] // parts).reshape((-1,) + (1,) * (len(dims) - 1 - dim))
    return loudness


def deal_out(key, own, number, rows, number_of, top, limit, lean):
    ranking = jax.random.permutation(key, number_of)
    heavy_load, ordinary = portions_of(number_of, rows * top, limit, lean, True), portions_of(number_of, rows * top, limit, lean, False)
    places = jnp.arange(number_of)

    def named(sizes, offset_by):
        used = int((sizes > 0).sum())
        fixed = max(1, used // 4)
        shifted = fixed + (places - fixed + offset_by * (used - fixed)) % max(1, number_of - fixed)
        return jnp.zeros((number_of,), jnp.int32).at[ranking[jnp.where(places < fixed, places, shifted)]].set(jnp.asarray(sizes, jnp.int32))

    sizes = jnp.where(number % 4 == 0, named(heavy_load, number // 4), named(ordinary, number - number // 4 - 1))
    mixed = jax.random.permutation(jax.random.fold_in(own, 3), number_of)
    source_of, receiver = mixed[0:number_of // 2 * 2:2], mixed[1:number_of // 2 * 2:2]
    margin = jnp.minimum(sizes[source_of] - 1, limit - sizes[receiver]) // 2
    margin = jnp.where((source_of == ranking[0]) | (receiver == ranking[0]) | (sizes[receiver] == 0), 0, jnp.maximum(margin, 0))
    shifted = jax.random.randint(jax.random.fold_in(own, 4), (number_of // 2,), 0, 1 << 20) % (margin + 1)
    sizes = sizes.at[source_of].add(-shifted).at[receiver].add(shifted)
    items = jnp.searchsorted(jnp.cumsum(sizes), jnp.arange(rows * top), side="right").astype(jnp.int32)
    grid = items.reshape(top, rows).T
    grid = grid[jax.random.permutation(jax.random.fold_in(own, 1), rows)]
    offset_by = jax.random.randint(jax.random.fold_in(own, 2), (rows, 1), 0, top)
    return jnp.take_along_axis(grid, (jnp.arange(top)[None, :] + offset_by) % top, axis=1)


def portions_of(count, total, reach, skew, full):
    portions = [(1 << 20) // math.isqrt(standing ** skew) + 1 for standing in range(1, count + 1)]
    largest = reach if full else min(reach, max(-(-total // count), total * portions[0] // sum(portions)))
    least = 1 if total - largest >= count - 1 else 0
    counts, rest = [largest] + [least] * (count - 1), total - largest - least * (count - 1)
    while rest > 0:
        movable = [i for i in range(1, count) if counts[i] < largest] or [i for i in range(1, count) if counts[i] < reach]
        mass, remaining = sum([portions[i] for i in movable]), rest
        for i in movable:
            extra = min(reach - counts[i], max(1, remaining * portions[i] // mass), rest)
            counts[i] = counts[i] + extra
            rest = rest - extra
    return np.array(counts)


def normal_values(stream_key, shape, spread, limit, shards=(), held_as=jnp.bfloat16):
    result = jax.random.normal(stream_key, shape, jnp.float32) * spread
    if len(shards) > 0:
        result = steps_of(stream_key, shape, shards, -0.22, 0.18) * result
    return jnp.clip(result, min=-limit, max=limit).astype(held_as)


def setup_inputs(seed: int = 0) -> dict:
    key_list = jax.random.split(jax.random.key(seed), 16)
    residual = normal_values(key_list[0], (TOKENS, D), 1.0, 6.0, ((0, 128),))
    prefill_qkv = draw_prefill_qkv(jax.random.fold_in(key_list[15], 71), 0)
    decode_qkv = draw_decode_qkv(jax.random.fold_in(key_list[15], 71), 0)
    cache_pool = draw_cache_pool(jax.random.fold_in(key_list[15], 71), 0)
    page_table = draw_page_table(jax.random.fold_in(key_list[15], 71), 0)
    cache_len = draw_cache_len(jax.random.fold_in(key_list[15], 71), 0)
    out_weight = normal_values(key_list[6], (D, D), D ** -0.5, 0.125, ((0, 16),))
    norm_gain = jnp.clip(1.0 + 0.18 * jax.random.normal(key_list[7], (D,), jnp.float32), 0.1, 1.9)
    shared_gate_up = normal_values(key_list[8], (2, D, FS), D ** -0.5, 0.125, ((2, 16),))
    shared_down = normal_values(key_list[9], (FS, D), FS ** -0.5, 0.078125, ((0, 16),))
    shared_gate = normal_values(key_list[10], (D,), (D // 4) ** -0.5, 0.25)
    routes_keys = jax.random.split(jax.random.fold_in(key_list[11], 1), TOKENS // T_DEV)
    routes_turns = jax.random.permutation(jax.random.fold_in(key_list[11], 3), TOKENS // T_DEV)
    routes = jax.vmap(lambda own, number: deal_out(jax.random.fold_in(key_list[11], 2), own, number, T_DEV, EXPERTS, TOPK, CAP, 2))(routes_keys, routes_turns).reshape((TOKENS, TOPK))
    route_weight = jnp.clip(0.1 + 0.4 * jax.random.uniform(key_list[12], (TOKENS, TOPK), jnp.float32) ** steps_of(key_list[12], (TOKENS, TOPK), ((0, 128),), -0.2, 0.2), 0.1, 0.5)
    expert_gate_up = normal_values(key_list[13], (SHARDS, 2, D, FE_DEV), D ** -0.5, 0.125, ((0, 128),))
    expert_down = normal_values(key_list[14], (SHARDS, FE_DEV, D), FE ** -0.5, 0.15625, ((0, 128),))
    return dict(residual=residual, prefill_qkv=prefill_qkv, decode_qkv=decode_qkv, cache_pool=cache_pool, page_table=page_table, cache_len=cache_len, out_weight=out_weight, norm_gain=norm_gain, shared_gate_up=shared_gate_up, shared_down=shared_down, shared_gate=shared_gate, routes=routes, route_weight=route_weight, expert_gate_up=expert_gate_up, expert_down=expert_down)


NEG_FILL = -1e+30

def masked_weights(scores, allowed):
    masked = jnp.where(allowed, scores, NEG_FILL)
    highest = lax.optimization_barrier(jnp.max(masked, axis=-1, keepdims=True))
    raised = jnp.where(allowed, jnp.exp(masked - highest), 0.0)
    return (raised / lax.optimization_barrier(jnp.sum(raised, axis=-1, keepdims=True))).astype(jnp.bfloat16)

def reference(residual, prefill_qkv, decode_qkv, cache_pool, page_table, cache_len, out_weight, norm_gain, shared_gate_up, shared_down, shared_gate, routes, route_weight, expert_gate_up, expert_down):
    scaling = HD ** (-0.5)

    def prefill_one(span_qkv):
        split_qkv = span_qkv.reshape(3, SPAN, HEADS, HD).astype(jnp.float32)
        scores = jnp.einsum('qhd,khd->hqk', split_qkv[0], split_qkv[1]) * scaling
        causal = jnp.arange(SPAN)[:, None] >= jnp.arange(SPAN)[None, :]
        weights = masked_weights(scores, causal[None])
        mixed_rows = jnp.einsum('hqk,khd->qhd', weights.astype(jnp.float32), split_qkv[2])
        return mixed_rows.reshape(SPAN, D).astype(jnp.bfloat16)

    def decode_one(operands):
        request_qkv, page_rows, length, position = operands
        device_row = position // DEC_DEV
        page_data = jnp.take(cache_pool, (device_row * PAGES_DEV + page_rows).astype(jnp.int32), axis=1)
        cache_keys = page_data[0].reshape(MAXLEN, HEADS, HD).astype(jnp.float32)
        cache_values = page_data[1].reshape(MAXLEN, HEADS, HD).astype(jnp.float32)
        query_row = request_qkv[0].reshape(HEADS, HD).astype(jnp.float32)
        own_key = request_qkv[1].reshape(HEADS, HD).astype(jnp.float32)
        own_value = request_qkv[2].reshape(HEADS, HD).astype(jnp.float32)
        cached = jnp.einsum('hd,thd->ht', query_row, cache_keys) * scaling
        own_score = lax.optimization_barrier(jnp.sum(query_row * own_key, axis=-1, keepdims=True)) * scaling
        joined = jnp.concatenate([cached, own_score], axis=1)
        live = jnp.arange(MAXLEN) < length
        allowed = jnp.concatenate([jnp.broadcast_to(live[None, :], (HEADS, MAXLEN)), jnp.ones((HEADS, 1), bool)], axis=1)
        weights = masked_weights(joined, allowed)
        mixed_rows = jnp.einsum('ht,thd->hd', weights[:, :MAXLEN].astype(jnp.float32), cache_values)
        mixed_rows = mixed_rows + weights[:, MAXLEN:].astype(jnp.float32) * own_value
        return mixed_rows.reshape(D).astype(jnp.bfloat16)
    prefill_out = lax.map(prefill_one, prefill_qkv)
    decode_out = lax.map(decode_one, (decode_qkv, page_table, cache_len, jnp.arange(DECODE).astype(jnp.int32)))
    attended = jnp.concatenate([prefill_out.reshape(N_REQ, PRE_DEV * SPAN, D), decode_out.reshape(N_REQ, DEC_DEV, D)], axis=1).reshape(TOKENS, D)
    projected = jnp.dot(attended, out_weight, preferred_element_type=jnp.float32)
    stream = lax.optimization_barrier((residual.astype(jnp.float32) + projected).astype(jnp.bfloat16))
    stream_wide = stream.astype(jnp.float32)
    normed = (stream_wide * lax.rsqrt(lax.optimization_barrier(jnp.mean(stream_wide * stream_wide, axis=-1, keepdims=True)) + 1e-06) * norm_gain).astype(jnp.bfloat16)
    gate_part = jnp.dot(normed, shared_gate_up[0], preferred_element_type=jnp.float32)
    up_part = jnp.dot(normed, shared_gate_up[1], preferred_element_type=jnp.float32)
    shared_hidden = (jax.nn.silu(gate_part) * up_part).astype(jnp.bfloat16)
    shared_out = jnp.zeros((TOKENS, D), jnp.float32)
    for block_index in range(N_EXP):
        lower = block_index * FS_DEV
        partial_value = jnp.dot(shared_hidden[:, lower:lower + FS_DEV], shared_down[lower:lower + FS_DEV], preferred_element_type=jnp.float32).astype(jnp.bfloat16)
        shared_out = shared_out + lax.optimization_barrier(partial_value).astype(jnp.float32)
    shared_scale = jax.nn.sigmoid(jnp.dot(normed, shared_gate, preferred_element_type=jnp.float32))
    flat_routes = routes.reshape(-1)
    flat_weights = route_weight.reshape(-1)
    token_ids = (jnp.arange(TOKENS * TOPK) // TOPK).astype(jnp.int32)
    slot_total = DEVICES * CAP

    def one_expert(running, operands):
        expert_id, gate_up, down_rows = operands
        hit_mask = flat_routes == expert_id
        slot_rank = jnp.cumsum(hit_mask.astype(jnp.int32)) - 1
        target = jnp.where(hit_mask, slot_rank, slot_total).astype(jnp.int32)
        slot_token = jnp.zeros((slot_total,), jnp.int32).at[target].set(token_ids, mode='drop')
        slot_weight = jnp.zeros((slot_total,), jnp.float32).at[target].set(flat_weights, mode='drop')
        gathered = normed[slot_token]
        expert_out = jnp.zeros((slot_total, D), jnp.float32)
        for shard_index in range(SPLIT):
            expert_gate = jnp.dot(gathered, gate_up[shard_index, 0], preferred_element_type=jnp.float32)
            expert_up = jnp.dot(gathered, gate_up[shard_index, 1], preferred_element_type=jnp.float32)
            hidden = (jax.nn.silu(expert_gate) * expert_up).astype(jnp.bfloat16)
            part_out = jnp.dot(hidden, down_rows[shard_index], preferred_element_type=jnp.float32).astype(jnp.bfloat16)
            expert_out = expert_out + lax.optimization_barrier(part_out).astype(jnp.float32)
        running = running.at[slot_token].add(slot_weight[:, None] * expert_out)
        return (running, expert_id)
    scanned = lax.scan(one_expert, jnp.zeros((TOKENS, D), jnp.float32), (jnp.arange(EXPERTS).astype(jnp.int32), expert_gate_up.reshape(EXPERTS, SPLIT, 2, D, FE_DEV), expert_down.reshape(EXPERTS, SPLIT, FE_DEV, D)))
    routed = scanned[0]
    layer_out = stream_wide + routed + shared_scale[:, None] * shared_out
    return layer_out.astype(jnp.bfloat16)
```

```python
import functools

import jax
import jax.numpy as jnp
from jax import lax
from jax.experimental import pallas as pl
from jax.experimental.pallas import tpu as pltpu
from jax.sharding import PartitionSpec as P

HD = 128
SIDE = 4
ROWS = 72
NEG_FILL = -1e30
MIB = 1 << 20
BF = jnp.bfloat16
F32 = jnp.float32
NT = (((1,), (1,)), ((), ()))


def vmem(limit):
    return pltpu.CompilerParams(vmem_limit_bytes=limit * MIB)


def dot(a, b):
    return jnp.dot(a, b, preferred_element_type=F32)


def attention_kernel(lens, table, pre, dec, pool, out, keys, values, scores, sems):
    scale = HD ** (-0.5)
    copies = [
        pltpu.make_async_copy(pool.at[i], buf, sems.at[i]) for i, buf in enumerate((keys, values))
    ]
    for c in copies:
        c.start()
    spans, _, span, _ = pre.shape
    part = span // 2
    for r in range(spans):
        for h in range(2):
            width = part * (h + 1)
            q = pre[r, 0, h * part : (h + 1) * part, :]
            k = pre[r, 1, :width, :]
            v = pre[r, 2, :width, :]
            s = lax.dot_general(q, k, NT, preferred_element_type=F32) * scale
            row = lax.broadcasted_iota(jnp.int32, s.shape, 0) + h * part
            col = lax.broadcasted_iota(jnp.int32, s.shape, 1)
            s = jnp.where(col <= row, s, NEG_FILL)
            p = jnp.exp(s - jnp.max(s, axis=-1, keepdims=True))
            w = (p / jnp.sum(p, axis=-1, keepdims=True)).astype(BF)
            out[r * span + h * part : r * span + (h + 1) * part, :] = dot(w, v).astype(BF)
    requests, entries = table.shape
    pages, page = keys.shape[0], keys.shape[1]
    held = jnp.clip(
        lens[...] - page * lax.broadcasted_iota(jnp.int32, (requests, entries), 1), 0, page
    )
    ids = table[...]
    lane = lax.broadcasted_iota(jnp.int32, (requests, page), 1)
    limit = jnp.zeros((requests, page), jnp.int32)
    for j in range(entries):
        limit = limit + jnp.where(ids[:, j : j + 1] == lane, held[:, j : j + 1], 0)
    q = dec[0]
    own = jnp.sum(q.astype(F32) * dec[1].astype(F32), axis=-1, keepdims=True) * scale
    group = 4
    wide = group * page
    copies[0].wait()
    top = jnp.full((requests, wide), NEG_FILL, F32)
    for c in range(pages // group):
        k = keys[c * group : (c + 1) * group].reshape(wide, HD)
        s = lax.dot_general(q, k, NT, preferred_element_type=F32) * scale
        s = jnp.concatenate(
            [
                jnp.where(
                    lane < limit[:, c * group + g : c * group + g + 1],
                    s[:, g * page : (g + 1) * page],
                    NEG_FILL,
                )
                for g in range(group)
            ],
            axis=1,
        )
        scores[:, c * wide : (c + 1) * wide] = s
        top = jnp.maximum(top, s)
    top = jnp.maximum(jnp.max(top, axis=-1, keepdims=True), own)
    total = jnp.zeros((requests, wide), F32)
    for c in range(pages // group):
        p = jnp.exp(scores[:, c * wide : (c + 1) * wide] - top)
        scores[:, c * wide : (c + 1) * wide] = p
        total = total + p
    own = jnp.exp(own - top)
    total = jnp.sum(total, axis=-1, keepdims=True) + own
    copies[1].wait()
    mixed = (own / total).astype(BF).astype(F32) * dec[2].astype(F32)
    for c in range(pages // group):
        w = (scores[:, c * wide : (c + 1) * wide] / total).astype(BF)
        mixed = mixed + dot(w, values[c * group : (c + 1) * group].reshape(wide, HD))
    out[spans * span : spans * span + requests, :] = mixed.astype(BF)


def attention(prefill_qkv, decode_qkv, cache_pool, page_table, cache_len):
    requests = decode_qkv.shape[0]
    pages, page = cache_pool.shape[1:3]
    rows = prefill_qkv.shape[0] * prefill_qkv.shape[2] + requests
    whole = pl.BlockSpec(memory_space=pltpu.VMEM)
    return pl.pallas_call(
        attention_kernel,
        out_shape=jax.ShapeDtypeStruct((rows, HD), BF),
        in_specs=[whole, whole, whole, whole, pl.BlockSpec(memory_space=pl.ANY)],
        out_specs=whole,
        scratch_shapes=[
            pltpu.VMEM((pages, page, HD), BF),
            pltpu.VMEM((pages, page, HD), BF),
            pltpu.VMEM((requests, pages * page), F32),
            pltpu.SemaphoreType.DMA((2,)),
        ],
        compiler_params=vmem(48),
        name="attention",
    )(cache_len[:, None], page_table, prefill_qkv, decode_qkv.transpose(1, 0, 2), cache_pool)


def project_kernel(mine, blocks, weight, *outs):
    half = weight.shape[1] // 2
    at_x, at_z = mine[0] // SIDE, mine[0] % SIDE

    def rows(picked):
        return jnp.concatenate([blocks[i].astype(F32) for i in picked], axis=0).astype(BF)

    xs = [jnp.bitwise_xor(at_x, d) * SIDE for d in range(SIDE)]
    zs = [jnp.bitwise_xor(at_z, d) for d in range(SIDE)]
    for d in range(SIDE):
        outs[d][...] = dot(rows([xs[d] + z for z in zs]), weight[:, :half]).astype(BF)
        outs[SIDE + d][...] = dot(rows([x + zs[d] for x in xs]), weight[:, half:]).astype(BF)


def project(attended, out_weight, mine):
    blocks = attended.reshape(SIDE * SIDE, -1, HD)
    blocks = jnp.pad(blocks, ((0, 0), (0, ROWS - blocks.shape[1]), (0, 0)))
    half = out_weight.shape[1] // 2
    whole = pl.BlockSpec(memory_space=pltpu.VMEM)
    return pl.pallas_call(
        project_kernel,
        out_shape=[jax.ShapeDtypeStruct((SIDE * ROWS, half), BF)] * (2 * SIDE),
        in_specs=[pl.BlockSpec(memory_space=pltpu.SMEM), whole, whole],
        out_specs=[whole] * (2 * SIDE),
        compiler_params=vmem(32),
        name="project",
    )(mine, blocks, out_weight)


def along_x(a, d):
    return lax.ppermute(a, "exp", [(i, i ^ (d * SIDE)) for i in range(SIDE * SIDE)])


def along_z(a, d):
    return lax.ppermute(a, "exp", [(i, i ^ d) for i in range(SIDE * SIDE)])


def add_up(parts):
    total = parts[0].astype(F32)
    for p in parts[1:]:
        total = total + p.astype(F32)
    return total


def reduce_scatter(parts):
    parts_a, parts_b = parts[:SIDE], parts[SIDE:]
    got_a, got_b = [parts_a[0]], [parts_b[0]]
    for d in (2, 1, 3):
        got_a.append(along_x(parts_a[d], d))
        got_b.append(along_z(parts_b[d], d))
    sum_a = add_up(got_a).astype(BF).reshape(SIDE, ROWS, -1)
    sum_b = add_up(got_b).astype(BF).reshape(SIDE, ROWS, -1)
    sum_a, sum_b = lax.optimization_barrier((sum_a, sum_b))
    got_a, got_b = [sum_a[0]], [sum_b[0]]
    for d in (2, 1, 3):
        got_a.append(along_z(sum_a[d], d))
        got_b.append(along_x(sum_b[d], d))
    return got_a, got_b


def token_kernel(a0, a1, a2, a3, b0, b1, b2, b3, residual, gain, select, stream, normed, outgoing):
    f = lambda r: r[...].astype(F32)
    projected = jnp.concatenate(
        [f(a0) + f(a1) + f(a2) + f(a3), f(b0) + f(b1) + f(b2) + f(b3)], axis=1
    )
    held = (f(residual) + projected).astype(BF)
    stream[...] = held
    wide = held.astype(F32)
    mean = jnp.mean(wide * wide, axis=-1, keepdims=True)
    rows = (wide * lax.rsqrt(mean + 1e-06) * gain[...]).astype(BF)
    normed[...] = rows
    experts, _, capacity, width = outgoing.shape
    group = 8
    for g in range(experts // group):
        n = group * capacity
        picked = dot(select[g * n : (g + 1) * n, :], rows).reshape(group, capacity, width).astype(BF)
        outgoing[g * group : (g + 1) * group, 0] = picked
        outgoing[g * group : (g + 1) * group, 1] = picked


def expert_kernel(rows, gate_up, down, out):
    x = rows[...]
    gate = dot(x, gate_up[0, 0])
    up = dot(x, gate_up[0, 1])
    hidden = (gate / (1.0 + jnp.exp(-gate)) * up).astype(BF)
    out[...] = dot(hidden, down[0]).astype(BF)


def experts(rows, gate_up, down):
    count, width = rows.shape
    step = 256
    return pl.pallas_call(
        expert_kernel,
        grid=(count // step,),
        out_shape=jax.ShapeDtypeStruct((count, width), BF),
        in_specs=[
            pl.BlockSpec((step, width), lambda i: (i, 0)),
            pl.BlockSpec(gate_up.shape, lambda i: (0, 0, 0, 0)),
            pl.BlockSpec(down.shape, lambda i: (0, 0, 0)),
        ],
        out_specs=pl.BlockSpec((step, width), lambda i: (i, 0)),
        compiler_params=vmem(40),
        cost_estimate=pl.CostEstimate(
            flops=6 * count * width * down.shape[1],
            bytes_accessed=2 * (2 * count * width + 3 * width * down.shape[1]),
            transcendentals=count * down.shape[1],
        ),
        name="experts",
    )(rows, gate_up, down)


def shared_kernel(mine, rows, gate_up, down, *rest):
    outs, hidden = rest[:-1], rest[-1]
    half = down.shape[1] // 2
    for g in range(SIDE):
        x = rows[g * SIDE * ROWS : (g + 1) * SIDE * ROWS, :]
        gate = dot(x, gate_up[0])
        up = dot(x, gate_up[1])
        hidden[g] = (gate / (1.0 + jnp.exp(-gate)) * up).reshape(SIDE, ROWS, -1)
    at_x, at_z = mine[0] // SIDE, mine[0] % SIDE
    for d in range(SIDE):
        x_row = jnp.bitwise_xor(at_x, d)
        z_row = jnp.bitwise_xor(at_z, d)
        part = jnp.concatenate([hidden[x_row, jnp.bitwise_xor(at_z, j)] for j in range(SIDE)], axis=0)
        outs[d][...] = dot(part.astype(BF), down[:, :half]).astype(BF)
        part = jnp.concatenate([hidden[jnp.bitwise_xor(at_x, j), z_row] for j in range(SIDE)], axis=0)
        outs[SIDE + d][...] = dot(part.astype(BF), down[:, half:]).astype(BF)


def shared_expert(mine, rows, gate_up, down):
    whole = pl.BlockSpec(memory_space=pltpu.VMEM)
    half = down.shape[1] // 2
    count, width = rows.shape
    return pl.pallas_call(
        shared_kernel,
        out_shape=[jax.ShapeDtypeStruct((SIDE * ROWS, half), BF)] * (2 * SIDE),
        in_specs=[pl.BlockSpec(memory_space=pltpu.SMEM), whole, whole, whole],
        out_specs=[whole] * (2 * SIDE),
        scratch_shapes=[pltpu.VMEM((SIDE, SIDE, ROWS, down.shape[0]), F32)],
        compiler_params=vmem(48),
        cost_estimate=pl.CostEstimate(
            flops=6 * count * width * down.shape[0],
            bytes_accessed=2 * (2 * count * width + 3 * width * down.shape[0]),
            transcendentals=count * down.shape[0],
        ),
        name="shared_expert",
    )(mine, rows, gate_up, down)


def on_device(
    residual,
    prefill_qkv,
    decode_qkv,
    cache_pool,
    page_table,
    cache_len,
    out_weight,
    norm_gain,
    shared_gate_up,
    shared_down,
    shared_gate,
    routes,
    route_weight,
    expert_gate_up,
    expert_down,
):
    mine = lax.axis_index("exp")
    groups = lax.axis_size("exp")
    tok_rows, width = residual.shape
    devices = groups * lax.axis_size("req")
    experts_all = devices // 2
    route_count = routes.shape[1]
    capacity = 8

    flat = routes.reshape(-1)
    place = jnp.arange(flat.shape[0], dtype=jnp.int32)
    same = (flat[:, None] == flat[None, :]) & (place[None, :] < place[:, None])
    rank = jnp.sum(same.astype(jnp.int32), axis=1)
    slot_of = (flat * capacity + rank).reshape(tok_rows, route_count)
    slot_of = jnp.pad(slot_of, ((0, ROWS - tok_rows), (0, 0)), constant_values=-1)
    weight = jnp.pad(route_weight, ((0, ROWS - tok_rows), (0, 0)))
    slots = jnp.arange(experts_all * capacity, dtype=jnp.int32)
    select = jnp.any(slots[:, None, None] == slot_of[None], axis=-1).astype(BF)
    columns = jnp.arange(devices * capacity, dtype=jnp.int32)
    columns = columns // (2 * capacity) * capacity + columns % capacity
    mix = jnp.sum(
        jnp.where(slot_of[:, :, None] == columns[None, None, :], weight[:, :, None], 0.0), axis=1
    )
    mix_high = mix.astype(BF)
    mix_low = (mix - mix_high.astype(F32)).astype(BF)
    mix = jnp.concatenate([mix_high, mix_low], axis=0)

    attended = attention(prefill_qkv, decode_qkv, cache_pool, page_table, cache_len)
    got_a, got_b = reduce_scatter(project(attended, out_weight, mine[None]))
    stream, normed, outgoing = pl.pallas_call(
        token_kernel,
        out_shape=[
            jax.ShapeDtypeStruct((ROWS, width), BF),
            jax.ShapeDtypeStruct((ROWS, width), BF),
            jax.ShapeDtypeStruct((experts_all, 2, capacity, width), BF),
        ],
        compiler_params=vmem(32),
        name="token_rows",
    )(
        *got_a,
        *got_b,
        jnp.pad(residual, ((0, ROWS - tok_rows), (0, 0))),
        norm_gain[None, :],
        select,
    )
    block_rows = lax.all_gather(normed, "exp", axis=0, tiled=True)
    arrived = lax.all_to_all(
        outgoing.reshape(devices, capacity, width),
        ("req", "exp"),
        split_axis=0,
        concat_axis=0,
        tiled=True,
    )
    answer = experts(arrived.reshape(devices * capacity, width), expert_gate_up, expert_down)
    returned = lax.all_to_all(
        answer.reshape(devices, capacity, width),
        ("req", "exp"),
        split_axis=0,
        concat_axis=0,
        tiled=True,
    )
    parts = shared_expert(mine[None], block_rows, shared_gate_up, shared_down)
    got_a, got_b = reduce_scatter(parts)
    shared = jnp.concatenate([add_up(got_a), add_up(got_b)], axis=1)
    shared_scale = jax.nn.sigmoid(dot(normed, shared_gate))
    routed = dot(mix, returned.reshape(devices * capacity, width))
    routed = routed[:ROWS] + routed[ROWS:]
    result = stream.astype(F32) + routed + shared_scale[:, None] * shared
    return result[:tok_rows].astype(BF)


def solution(mesh):
    placed = (
        P(("req", "exp"), None),
        P("req", None, None, "exp"),
        P("req", None, "exp"),
        P(None, "req", None, "exp"),
        P("req", None),
        P("req"),
        P("exp", None),
        P(),
        P(None, None, "exp"),
        P("exp", None),
        P(),
        P(("req", "exp"), None),
        P(("req", "exp"), None),
        P(("req", "exp"), None, None, None),
        P(("req", "exp"), None, None),
    )
    return jax.shard_map(
        on_device, mesh=mesh, in_specs=placed, out_specs=P(("req", "exp"), None), check_vma=False
    )
```

```python
import functools

import jax
import jax.numpy as jnp
from jax import lax
from jax.experimental import pallas as pl
from jax.experimental.pallas import tpu as pltpu
from jax.sharding import PartitionSpec as P

HD = 128
SIDE = 4
ROWS = 72
NEG_FILL = -1e30
MIB = 1 << 20
BF = jnp.bfloat16
F32 = jnp.float32
NT = (((1,), (1,)), ((), ()))


def vmem(limit):
    return pltpu.CompilerParams(vmem_limit_bytes=limit * MIB)


def dot(a, b):
    return jnp.dot(a, b, preferred_element_type=F32)


def attention_kernel(lens, table, pre, dec, pool, out, keys, values, scores, sems):
    scale = HD ** (-0.5)
    copies = [
        pltpu.make_async_copy(pool.at[i], buf, sems.at[i]) for i, buf in enumerate((keys, values))
    ]
    for c in copies:
        c.start()
    spans, _, span, _ = pre.shape
    part = span // 2
    for r in range(spans):
        for h in range(2):
            width = part * (h + 1)
            q = pre[r, 0, h * part : (h + 1) * part, :]
            k = pre[r, 1, :width, :]
            v = pre[r, 2, :width, :]
            s = lax.dot_general(q, k, NT, preferred_element_type=F32) * scale
            row = lax.broadcasted_iota(jnp.int32, s.shape, 0) + h * part
            col = lax.broadcasted_iota(jnp.int32, s.shape, 1)
            s = jnp.where(col <= row, s, NEG_FILL)
            p = jnp.exp(s - jnp.max(s, axis=-1, keepdims=True))
            w = (p / jnp.sum(p, axis=-1, keepdims=True)).astype(BF)
            out[r * span + h * part : r * span + (h + 1) * part, :] = dot(w, v).astype(BF)
    requests, entries = table.shape
    pages, page = keys.shape[0], keys.shape[1]
    held = jnp.clip(
        lens[...] - page * lax.broadcasted_iota(jnp.int32, (requests, entries), 1), 0, page
    )
    ids = table[...]
    lane = lax.broadcasted_iota(jnp.int32, (requests, page), 1)
    limit = jnp.zeros((requests, page), jnp.int32)
    for j in range(entries):
        limit = limit + jnp.where(ids[:, j : j + 1] == lane, held[:, j : j + 1], 0)
    q = dec[0]
    own = jnp.sum(q.astype(F32) * dec[1].astype(F32), axis=-1, keepdims=True) * scale
    group = 4
    wide = group * page
    copies[0].wait()
    top = jnp.full((requests, wide), NEG_FILL, F32)
    for c in range(pages // group):
        k = keys[c * group : (c + 1) * group].reshape(wide, HD)
        s = lax.dot_general(q, k, NT, preferred_element_type=F32) * scale
        s = jnp.concatenate(
            [
                jnp.where(
                    lane < limit[:, c * group + g : c * group + g + 1],
                    s[:, g * page : (g + 1) * page],
                    NEG_FILL,
                )
                for g in range(group)
            ],
            axis=1,
        )
        scores[:, c * wide : (c + 1) * wide] = s
        top = jnp.maximum(top, s)
    top = jnp.maximum(jnp.max(top, axis=-1, keepdims=True), own)
    total = jnp.zeros((requests, wide), F32)
    for c in range(pages // group):
        p = jnp.exp(scores[:, c * wide : (c + 1) * wide] - top)
        scores[:, c * wide : (c + 1) * wide] = p
        total = total + p
    own = jnp.exp(own - top)
    total = jnp.sum(total, axis=-1, keepdims=True) + own
    copies[1].wait()
    mixed = (own / total).astype(BF).astype(F32) * dec[2].astype(F32)
    for c in range(pages // group):
        w = (scores[:, c * wide : (c + 1) * wide] / total).astype(BF)
        mixed = mixed + dot(w, values[c * group : (c + 1) * group].reshape(wide, HD))
    out[spans * span : spans * span + requests, :] = mixed.astype(BF)


def attention(prefill_qkv, decode_qkv, cache_pool, page_table, cache_len):
    requests = decode_qkv.shape[0]
    pages, page = cache_pool.shape[1:3]
    rows = prefill_qkv.shape[0] * prefill_qkv.shape[2] + requests
    whole = pl.BlockSpec(memory_space=pltpu.VMEM)
    return pl.pallas_call(
        attention_kernel,
        out_shape=jax.ShapeDtypeStruct((rows, HD), BF),
        in_specs=[whole, whole, whole, whole, pl.BlockSpec(memory_space=pl.ANY)],
        out_specs=whole,
        scratch_shapes=[
            pltpu.VMEM((pages, page, HD), BF),
            pltpu.VMEM((pages, page, HD), BF),
            pltpu.VMEM((requests, pages * page), F32),
            pltpu.SemaphoreType.DMA((2,)),
        ],
        compiler_params=vmem(48),
        name="attention",
    )(cache_len[:, None], page_table, prefill_qkv, decode_qkv.transpose(1, 0, 2), cache_pool)


def project_kernel(mine, blocks, weight, *outs):
    half = weight.shape[1] // 2
    at_x, at_z = mine[0] // SIDE, mine[0] % SIDE

    def rows(picked):
        return jnp.concatenate([blocks[i].astype(F32) for i in picked], axis=0).astype(BF)

    xs = [jnp.bitwise_xor(at_x, d) * SIDE for d in range(SIDE)]
    zs = [jnp.bitwise_xor(at_z, d) for d in range(SIDE)]
    for d in range(SIDE):
        outs[d][...] = dot(rows([xs[d] + z for z in zs]), weight[:, :half]).astype(BF)
        outs[SIDE + d][...] = dot(rows([x + zs[d] for x in xs]), weight[:, half:]).astype(BF)


def project(attended, out_weight, mine):
    blocks = attended.reshape(SIDE * SIDE, -1, HD)
    blocks = jnp.pad(blocks, ((0, 0), (0, ROWS - blocks.shape[1]), (0, 0)))
    half = out_weight.shape[1] // 2
    whole = pl.BlockSpec(memory_space=pltpu.VMEM)
    return pl.pallas_call(
        project_kernel,
        out_shape=[jax.ShapeDtypeStruct((SIDE * ROWS, half), BF)] * (2 * SIDE),
        in_specs=[pl.BlockSpec(memory_space=pltpu.SMEM), whole, whole],
        out_specs=[whole] * (2 * SIDE),
        compiler_params=vmem(32),
        name="project",
    )(mine, blocks, out_weight)


def along_x(a, d):
    return lax.ppermute(a, "exp", [(i, i ^ (d * SIDE)) for i in range(SIDE * SIDE)])


def along_z(a, d):
    return lax.ppermute(a, "exp", [(i, i ^ d) for i in range(SIDE * SIDE)])


def add_up(parts):
    total = parts[0].astype(F32)
    for p in parts[1:]:
        total = total + p.astype(F32)
    return total


def sum_first(parts):
    parts_a, parts_b = parts[:SIDE], parts[SIDE:]
    got_a, got_b = [parts_a[0]], [parts_b[0]]
    for d in (1, 3, 2):
        got_a.append(along_x(parts_a[d], d))
        got_b.append(along_z(parts_b[d], d))
    sum_a = add_up(got_a).astype(BF).reshape(SIDE, ROWS, -1)
    sum_b = add_up(got_b).astype(BF).reshape(SIDE, ROWS, -1)
    return sum_a, sum_b


def sum_second(sum_a, sum_b):
    got_a, got_b = [sum_a[0]], [sum_b[0]]
    for d in (1, 3, 2):
        got_a.append(along_z(sum_a[d], d))
        got_b.append(along_x(sum_b[d], d))
    return got_a, got_b


def gather(rows):
    half = rows.shape[1] // 2
    rows_a, rows_b = rows[:, :half], rows[:, half:]
    got_a, got_b = {0: rows_a}, {0: rows_b}
    for d in (1, 3, 2):
        got_a[d] = along_z(rows_a, d)
        got_b[d] = along_x(rows_b, d)
    rows_a = jnp.stack([got_a[d] for d in range(SIDE)])
    rows_b = jnp.stack([got_b[d] for d in range(SIDE)])
    rows_a, rows_b = lax.optimization_barrier((rows_a, rows_b))
    got_a, got_b = {0: rows_a}, {0: rows_b}
    for d in (1, 3, 2):
        got_a[d] = along_x(rows_a, d)
        got_b[d] = along_z(rows_b, d)
    return [got_a[d] for d in range(SIDE)], [got_b[d] for d in range(SIDE)]


def token_kernel(a0, a1, a2, a3, b0, b1, b2, b3, residual, gain, stream, normed):
    f = lambda r: r[...].astype(F32)
    projected = jnp.concatenate(
        [f(a0) + f(a1) + f(a2) + f(a3), f(b0) + f(b1) + f(b2) + f(b3)], axis=1
    )
    held = (f(residual) + projected).astype(BF)
    stream[...] = held
    wide = held.astype(F32)
    mean = jnp.mean(wide * wide, axis=-1, keepdims=True)
    normed[...] = (wide * lax.rsqrt(mean + 1e-06) * gain[...]).astype(BF)


def pick_kernel(mine, *refs):
    rows_a, rows_b, select, out = refs[:SIDE], refs[SIDE : 2 * SIDE], refs[-2], refs[-1]
    columns, _, capacity, width = out.shape
    half = width // 2
    for x in range(SIDE):
        for z in range(SIDE):
            block = jnp.bitwise_xor(mine[0], x * SIDE + z)
            chosen = select[block]
            a = dot(chosen, rows_a[x][z]).reshape(columns, capacity, half).astype(BF)
            b = dot(chosen, rows_b[z][x]).reshape(columns, capacity, half).astype(BF)
            for r in range(columns):
                out[r, block, :, :half] = a[r]
                out[r, block, :, half:] = b[r]


def pick(mine, rows_a, rows_b, select, capacity):
    blocks, slots, _ = select.shape
    width = 2 * rows_a[0].shape[-1]
    whole = pl.BlockSpec(memory_space=pltpu.VMEM)
    return pl.pallas_call(
        pick_kernel,
        out_shape=jax.ShapeDtypeStruct((slots // capacity, blocks, capacity, width), BF),
        in_specs=[pl.BlockSpec(memory_space=pltpu.SMEM)] + [whole] * (2 * SIDE + 1),
        out_specs=whole,
        compiler_params=vmem(32),
        name="pick",
    )(mine, *rows_a, *rows_b, select)


def expert_kernel(rows, gate_up, down, out):
    x = rows[...]
    gate = dot(x, gate_up[0, 0])
    up = dot(x, gate_up[0, 1])
    hidden = (gate / (1.0 + jnp.exp(-gate)) * up).astype(BF)
    out[...] = dot(hidden, down[0]).astype(BF)


def experts(rows, gate_up, down):
    count, width = rows.shape
    step = 256
    return pl.pallas_call(
        expert_kernel,
        grid=(count // step,),
        out_shape=jax.ShapeDtypeStruct((count, width), BF),
        in_specs=[
            pl.BlockSpec((step, width), lambda i: (i, 0)),
            pl.BlockSpec(gate_up.shape, lambda i: (0, 0, 0, 0)),
            pl.BlockSpec(down.shape, lambda i: (0, 0, 0)),
        ],
        out_specs=pl.BlockSpec((step, width), lambda i: (i, 0)),
        compiler_params=vmem(40),
        cost_estimate=pl.CostEstimate(
            flops=6 * count * width * down.shape[1],
            bytes_accessed=2 * (2 * count * width + 3 * width * down.shape[1]),
            transcendentals=count * down.shape[1],
        ),
        name="experts",
    )(rows, gate_up, down)


def shared_kernel(*refs):
    rows_a, rows_b = refs[:SIDE], refs[SIDE : 2 * SIDE]
    gate_up, down = refs[2 * SIDE : 2 * SIDE + 2]
    outs, hidden = refs[2 * SIDE + 2 : -1], refs[-1]
    half = down.shape[1] // 2
    for x in range(SIDE):
        a = rows_a[x][...]
        b = jnp.concatenate(
            [rows_b[z][x].astype(F32) for z in range(SIDE)], axis=0
        ).astype(BF)
        gate = dot(a, gate_up[0, :half]) + dot(b, gate_up[0, half:])
        up = dot(a, gate_up[1, :half]) + dot(b, gate_up[1, half:])
        hidden[x] = (gate / (1.0 + jnp.exp(-gate)) * up).reshape(SIDE, ROWS, -1)
    for d in range(SIDE):
        part = hidden[d].reshape(SIDE * ROWS, -1)
        outs[d][...] = dot(part.astype(BF), down[:, :half]).astype(BF)
        part = hidden[:, d].reshape(SIDE * ROWS, -1)
        outs[SIDE + d][...] = dot(part.astype(BF), down[:, half:]).astype(BF)


def shared_expert(rows_a, rows_b, gate_up, down):
    half = down.shape[1] // 2
    count, width = SIDE * SIDE * ROWS, down.shape[1]
    return pl.pallas_call(
        shared_kernel,
        out_shape=[jax.ShapeDtypeStruct((SIDE * ROWS, half), BF)] * (2 * SIDE),
        scratch_shapes=[pltpu.VMEM((SIDE, SIDE, ROWS, down.shape[0]), F32)],
        compiler_params=vmem(48),
        cost_estimate=pl.CostEstimate(
            flops=6 * count * width * down.shape[0],
            bytes_accessed=2 * (2 * count * width + 3 * width * down.shape[0]),
            transcendentals=count * down.shape[0],
        ),
        name="shared_expert",
    )(*[a.reshape(SIDE * ROWS, half) for a in rows_a], *rows_b, gate_up, down)


def on_device(
    residual,
    prefill_qkv,
    decode_qkv,
    cache_pool,
    page_table,
    cache_len,
    out_weight,
    norm_gain,
    shared_gate_up,
    shared_down,
    shared_gate,
    routes,
    route_weight,
    expert_gate_up,
    expert_down,
):
    mine = lax.axis_index("exp")
    groups = lax.axis_size("exp")
    tok_rows, width = residual.shape
    devices = groups * lax.axis_size("req")
    experts_all = devices // 2
    route_count = routes.shape[1]
    capacity = 8

    flat = routes.reshape(-1)
    place = jnp.arange(flat.shape[0], dtype=jnp.int32)
    same = (flat[:, None] == flat[None, :]) & (place[None, :] < place[:, None])
    rank = jnp.sum(same.astype(jnp.int32), axis=1)
    slot_of = (flat * capacity + rank).reshape(tok_rows, route_count)
    slot_of = jnp.pad(slot_of, ((0, ROWS - tok_rows), (0, 0)), constant_values=-1)
    weight = jnp.pad(route_weight, ((0, ROWS - tok_rows), (0, 0)))
    block_routes = jnp.pad(
        lax.all_gather(routes, "exp", axis=0),
        ((0, 0), (0, ROWS - tok_rows), (0, 0)),
        constant_values=-1,
    )
    split = experts_all // lax.axis_size("req")
    column = jnp.arange(lax.axis_size("req"), dtype=jnp.int32) * split + mine // 2
    hit = jnp.any(block_routes[:, None] == column[None, :, None, None], axis=-1)
    before = jnp.arange(ROWS)[:, None] < jnp.arange(ROWS)[None, :]
    hit_rank = dot(hit.astype(BF), before.astype(BF)).astype(jnp.int32)
    select = hit[:, :, None] & (hit_rank[:, :, None] == jnp.arange(capacity)[None, None, :, None])
    select = select.astype(BF).reshape(groups, -1, ROWS)
    columns = jnp.arange(devices * capacity, dtype=jnp.int32)
    columns = columns // (2 * capacity) * capacity + columns % capacity
    mix = jnp.sum(
        jnp.where(slot_of[:, :, None] == columns[None, None, :], weight[:, :, None], 0.0), axis=1
    )
    mix_high = mix.astype(BF)
    mix_low = (mix - mix_high.astype(F32)).astype(BF)
    mix = jnp.concatenate([mix_high, mix_low], axis=0)

    attended = attention(prefill_qkv, decode_qkv, cache_pool, page_table, cache_len)
    sums = sum_first(project(attended, out_weight, mine[None]))
    got_a, got_b = sum_second(*lax.optimization_barrier(sums))
    stream, normed = pl.pallas_call(
        token_kernel,
        out_shape=[jax.ShapeDtypeStruct((ROWS, width), BF)] * 2,
        compiler_params=vmem(32),
        name="token_rows",
    )(*got_a, *got_b, jnp.pad(residual, ((0, ROWS - tok_rows), (0, 0))), norm_gain[None, :])
    rows_a, rows_b = gather(normed)
    outgoing = pick(mine[None], rows_a, rows_b, select, capacity)
    arrived = lax.all_to_all(
        outgoing.reshape(lax.axis_size("req"), groups * capacity, width),
        "req",
        split_axis=0,
        concat_axis=0,
        tiled=True,
    )
    sums = sum_first(shared_expert(rows_a, rows_b, shared_gate_up, shared_down))
    arrived, *sums = lax.optimization_barrier((arrived, *sums))
    got_a, got_b = sum_second(*sums)
    answer = experts(arrived.reshape(devices * capacity, width), expert_gate_up, expert_down)
    answer, got_a, got_b = lax.optimization_barrier((answer, got_a, got_b))
    returned = lax.all_to_all(
        answer.reshape(devices, capacity, width),
        ("req", "exp"),
        split_axis=0,
        concat_axis=0,
        tiled=True,
    )
    shared = jnp.concatenate([add_up(got_a), add_up(got_b)], axis=1)
    shared_scale = jax.nn.sigmoid(dot(normed, shared_gate))
    routed = dot(mix, returned.reshape(devices * capacity, width))
    routed = routed[:ROWS] + routed[ROWS:]
    result = stream.astype(F32) + routed + shared_scale[:, None] * shared
    return result[:tok_rows].astype(BF)


def solution(mesh):
    placed = (
        P(("req", "exp"), None),
        P("req", None, None, "exp"),
        P("req", None, "exp"),
        P(None, "req", None, "exp"),
        P("req", None),
        P("req"),
        P("exp", None),
        P(),
        P(None, None, "exp"),
        P("exp", None),
        P(),
        P(("req", "exp"), None),
        P(("req", "exp"), None),
        P(("req", "exp"), None, None, None),
        P(("req", "exp"), None, None),
    )
    return jax.shard_map(
        on_device, mesh=mesh, in_specs=placed, out_specs=P(("req", "exp"), None), check_vma=False
    )
```

```python
import functools

import jax
import jax.numpy as jnp
from jax import lax
from jax.experimental import pallas as pl
from jax.experimental.pallas import tpu as pltpu
from jax.sharding import PartitionSpec as P

HD = 128
SIDE = 4
TOKENS = 65
ROWS = 72
LANES = 128
ROUTES = 4
NEG_FILL = -1e30
MIB = 1 << 20
BF = jnp.bfloat16
F32 = jnp.float32
NT = (((1,), (1,)), ((), ()))


def vmem(limit):
    return pltpu.CompilerParams(vmem_limit_bytes=limit * MIB)


def dot(a, b):
    return jnp.dot(a, b, preferred_element_type=F32)


def dot_nt(a, b):
    return lax.dot_general(a, b, NT, preferred_element_type=F32)


def attention_kernel(lens, table, pre, dec, pool, out, keys, values, scores, sems):
    scale = HD ** (-0.5)
    copies = [
        pltpu.make_async_copy(pool.at[i], buf, sems.at[i]) for i, buf in enumerate((keys, values))
    ]
    for c in copies:
        c.start()
    spans, _, span, _ = pre.shape
    part = span // 2
    for r in range(spans):
        for h in range(2):
            width = part * (h + 1)
            q = pre[r, 0, h * part : (h + 1) * part, :]
            k = pre[r, 1, :width, :]
            v = pre[r, 2, :width, :]
            s = lax.dot_general(q, k, NT, preferred_element_type=F32) * scale
            row = lax.broadcasted_iota(jnp.int32, s.shape, 0) + h * part
            col = lax.broadcasted_iota(jnp.int32, s.shape, 1)
            s = jnp.where(col <= row, s, NEG_FILL)
            p = jnp.exp(s - jnp.max(s, axis=-1, keepdims=True))
            w = (p / jnp.sum(p, axis=-1, keepdims=True)).astype(BF)
            out[r * span + h * part : r * span + (h + 1) * part, :] = dot(w, v).astype(BF)
    requests, entries = table.shape
    pages, page = keys.shape[0], keys.shape[1]
    held = jnp.clip(
        lens[...] - page * lax.broadcasted_iota(jnp.int32, (requests, entries), 1), 0, page
    )
    ids = table[...]
    lane = lax.broadcasted_iota(jnp.int32, (requests, page), 1)
    limit = jnp.zeros((requests, page), jnp.int32)
    for j in range(entries):
        limit = limit + jnp.where(ids[:, j : j + 1] == lane, held[:, j : j + 1], 0)
    q = dec[0]
    own = jnp.sum(q.astype(F32) * dec[1].astype(F32), axis=-1, keepdims=True) * scale
    group = 4
    wide = group * page
    copies[0].wait()
    top = jnp.full((requests, wide), NEG_FILL, F32)
    for c in range(pages // group):
        k = keys[c * group : (c + 1) * group].reshape(wide, HD)
        s = lax.dot_general(q, k, NT, preferred_element_type=F32) * scale
        s = jnp.concatenate(
            [
                jnp.where(
                    lane < limit[:, c * group + g : c * group + g + 1],
                    s[:, g * page : (g + 1) * page],
                    NEG_FILL,
                )
                for g in range(group)
            ],
            axis=1,
        )
        scores[:, c * wide : (c + 1) * wide] = s
        top = jnp.maximum(top, s)
    top = jnp.maximum(jnp.max(top, axis=-1, keepdims=True), own)
    total = jnp.zeros((requests, wide), F32)
    for c in range(pages // group):
        p = jnp.exp(scores[:, c * wide : (c + 1) * wide] - top)
        scores[:, c * wide : (c + 1) * wide] = p
        total = total + p
    own = jnp.exp(own - top)
    total = jnp.sum(total, axis=-1, keepdims=True) + own
    copies[1].wait()
    mixed = (own / total).astype(BF).astype(F32) * dec[2].astype(F32)
    for c in range(pages // group):
        w = (scores[:, c * wide : (c + 1) * wide] / total).astype(BF)
        mixed = mixed + dot(w, values[c * group : (c + 1) * group].reshape(wide, HD))
    out[spans * span : spans * span + requests, :] = mixed.astype(BF)


def attention(prefill_qkv, decode_qkv, cache_pool, page_table, cache_len):
    requests = decode_qkv.shape[0]
    pages, page = cache_pool.shape[1:3]
    rows = prefill_qkv.shape[0] * prefill_qkv.shape[2] + requests
    whole = pl.BlockSpec(memory_space=pltpu.VMEM)
    return pl.pallas_call(
        attention_kernel,
        out_shape=jax.ShapeDtypeStruct((rows, HD), BF),
        in_specs=[whole, whole, whole, whole, pl.BlockSpec(memory_space=pl.ANY)],
        out_specs=whole,
        scratch_shapes=[
            pltpu.VMEM((pages, page, HD), BF),
            pltpu.VMEM((pages, page, HD), BF),
            pltpu.VMEM((requests, pages * page), F32),
            pltpu.SemaphoreType.DMA((2,)),
        ],
        compiler_params=vmem(48),
        name="attention",
    )(cache_len[:, None], page_table, prefill_qkv, decode_qkv.transpose(1, 0, 2), cache_pool)


def project_kernel(mine, blocks, weight, *outs):
    half = weight.shape[1] // 2
    at_x, at_z = mine[0] // SIDE, mine[0] % SIDE

    def rows(picked):
        return jnp.concatenate([blocks[i].astype(F32) for i in picked], axis=0).astype(BF)

    xs = [jnp.bitwise_xor(at_x, d) * SIDE for d in range(SIDE)]
    zs = [jnp.bitwise_xor(at_z, d) for d in range(SIDE)]
    for d in range(SIDE):
        outs[d][...] = dot(rows([xs[d] + z for z in zs]), weight[:, :half]).astype(BF)
        outs[SIDE + d][...] = dot(rows([x + zs[d] for x in xs]), weight[:, half:]).astype(BF)


def project(attended, out_weight, mine):
    blocks = attended.reshape(SIDE * SIDE, -1, HD)
    blocks = jnp.pad(blocks, ((0, 0), (0, ROWS - blocks.shape[1]), (0, 0)))
    half = out_weight.shape[1] // 2
    whole = pl.BlockSpec(memory_space=pltpu.VMEM)
    return pl.pallas_call(
        project_kernel,
        out_shape=[jax.ShapeDtypeStruct((SIDE * ROWS, half), BF)] * (2 * SIDE),
        in_specs=[pl.BlockSpec(memory_space=pltpu.SMEM), whole, whole],
        out_specs=[whole] * (2 * SIDE),
        compiler_params=vmem(32),
        name="project",
    )(mine, blocks, out_weight)


def along_x(a, d):
    return lax.ppermute(a, "exp", [(i, i ^ (d * SIDE)) for i in range(SIDE * SIDE)])


def along_z(a, d):
    return lax.ppermute(a, "exp", [(i, i ^ d) for i in range(SIDE * SIDE)])


def add_up(parts):
    total = parts[0].astype(F32)
    for p in parts[1:]:
        total = total + p.astype(F32)
    return total


def sum_first(parts):
    parts_a, parts_b = parts[:SIDE], parts[SIDE:]
    got_a, got_b = [parts_a[0]], [parts_b[0]]
    for d in (1, 3, 2):
        got_a.append(along_x(parts_a[d], d))
        got_b.append(along_z(parts_b[d], d))
    sum_a = add_up(got_a).astype(BF).reshape(SIDE, ROWS, -1)
    sum_b = add_up(got_b).astype(BF).reshape(SIDE, ROWS, -1)
    return sum_a, sum_b


def sum_second(sum_a, sum_b):
    got_a, got_b = [sum_a[0]], [sum_b[0]]
    for d in (1, 3, 2):
        got_a.append(along_z(sum_a[d], d))
        got_b.append(along_x(sum_b[d], d))
    return got_a, got_b


def gather(rows):
    half = rows.shape[1] // 2
    rows_a, rows_b = rows[:, :half], rows[:, half:]
    got_a, got_b = {0: rows_a}, {0: rows_b}
    for d in (1, 3, 2):
        got_a[d] = along_z(rows_a, d)
        got_b[d] = along_x(rows_b, d)
    rows_a = jnp.stack([got_a[d] for d in range(SIDE)])
    rows_b = jnp.stack([got_b[d] for d in range(SIDE)])
    rows_a, rows_b = lax.optimization_barrier((rows_a, rows_b))
    got_a, got_b = {0: rows_a}, {0: rows_b}
    for d in (1, 3, 2):
        got_a[d] = along_x(rows_a, d)
        got_b[d] = along_z(rows_b, d)
    return [got_a[d] for d in range(SIDE)], [got_b[d] for d in range(SIDE)]


def token_kernel(a0, a1, a2, a3, b0, b1, b2, b3, residual, gain, tags, stream, normed):
    f = lambda r: r[...].astype(F32)
    projected = jnp.concatenate(
        [f(a0) + f(a1) + f(a2) + f(a3), f(b0) + f(b1) + f(b2) + f(b3)], axis=1
    )
    held = (f(residual) + projected).astype(BF)
    stream[...] = held
    wide = held.astype(F32)
    mean = jnp.mean(wide * wide, axis=-1, keepdims=True)
    rows = wide * lax.rsqrt(mean + 1e-06) * gain[...]
    normed[...] = rows.astype(BF)
    count, lanes = tags.shape
    is_tag = lax.broadcasted_iota(jnp.int32, (count, lanes), 0) >= TOKENS
    normed[:, :lanes] = jnp.where(is_tag, tags[...], rows[:, :lanes]).astype(BF)


def chosen_rows(mine, rows_a, columns, capacity):
    shape = (columns, LANES)
    expert = lax.broadcasted_iota(jnp.int32, shape, 0) * (SIDE * SIDE // 2) + mine // 2
    expert = expert.astype(F32)
    hits = []
    for x in range(SIDE):
        for z in range(SIDE):
            tags = rows_a[x][z][:, :LANES].astype(F32)
            hit = jnp.zeros(shape, F32)
            for k in range(ROUTES):
                named = jnp.broadcast_to(tags[TOKENS + k : TOKENS + k + 1, :], shape)
                hit = jnp.where(named == expert, 1.0, hit)
            hits.append(hit)
    hits = jnp.concatenate(hits, axis=0)
    before = lax.broadcasted_iota(jnp.int32, (LANES, LANES), 0) < lax.broadcasted_iota(
        jnp.int32, (LANES, LANES), 1
    )
    rank = dot(hits.astype(BF), before.astype(F32).astype(BF))
    rank = jnp.where(hits > 0.0, rank, -1.0)
    slot = lax.broadcasted_iota(jnp.int32, (columns, capacity, LANES), 1).astype(F32)
    chosen = []
    for i in range(SIDE * SIDE):
        here = rank[i * columns : (i + 1) * columns, :]
        here = jnp.broadcast_to(here[:, None, :], (columns, capacity, LANES))
        here = jnp.where(here == slot, 1.0, 0.0).reshape(columns * capacity, LANES)
        chosen.append(here[:, :ROWS].astype(BF))
    return chosen


def pick_kernel(mine, *refs):
    rows_a, rows_b, out = refs[:SIDE], refs[SIDE : 2 * SIDE], refs[-1]
    columns, _, capacity, width = out.shape
    half = width // 2
    chosen = chosen_rows(mine[0], rows_a, columns, capacity)
    for x in range(SIDE):
        for z in range(SIDE):
            block = jnp.bitwise_xor(mine[0], x * SIDE + z)
            pick = chosen[x * SIDE + z]
            a = dot(pick, rows_a[x][z]).reshape(columns, capacity, half).astype(BF)
            b = dot(pick, rows_b[z][x]).reshape(columns, capacity, half).astype(BF)
            for r in range(columns):
                out[r, block, :, :half] = a[r]
                out[r, block, :, half:] = b[r]


def pick(mine, rows_a, rows_b, columns, capacity):
    width = 2 * rows_a[0].shape[-1]
    whole = pl.BlockSpec(memory_space=pltpu.VMEM)
    return pl.pallas_call(
        pick_kernel,
        out_shape=jax.ShapeDtypeStruct((columns, SIDE * SIDE, capacity, width), BF),
        in_specs=[pl.BlockSpec(memory_space=pltpu.SMEM)] + [whole] * (2 * SIDE),
        out_specs=whole,
        compiler_params=vmem(56),
        name="pick",
    )(mine, *rows_a, *rows_b)


def expert_kernel(rows, gate_up, down, out):
    x = rows[...]
    gate = dot_nt(x, gate_up[0, 0])
    up = dot_nt(x, gate_up[0, 1])
    hidden = (gate / (1.0 + jnp.exp(-gate)) * up).astype(BF)
    out[...] = dot(hidden, down[0]).astype(BF)


def experts(rows, gate_up, down):
    count, width = rows.shape
    step = 256
    return pl.pallas_call(
        expert_kernel,
        grid=(count // step,),
        out_shape=jax.ShapeDtypeStruct((count, width), BF),
        in_specs=[
            pl.BlockSpec((step, width), lambda i: (i, 0)),
            pl.BlockSpec(gate_up.shape, lambda i: (0, 0, 0, 0)),
            pl.BlockSpec(down.shape, lambda i: (0, 0, 0)),
        ],
        out_specs=pl.BlockSpec((step, width), lambda i: (i, 0)),
        compiler_params=vmem(50),
        cost_estimate=pl.CostEstimate(
            flops=6 * count * width * down.shape[1],
            bytes_accessed=2 * (2 * count * width + 3 * width * down.shape[1]),
            transcendentals=count * down.shape[1],
        ),
        name="experts",
    )(rows, gate_up, down)


def shared_kernel(*refs):
    rows_a, rows_b = refs[:SIDE], refs[SIDE : 2 * SIDE]
    gate_up, down = refs[2 * SIDE : 2 * SIDE + 2]
    outs, hidden = refs[2 * SIDE + 2 : -1], refs[-1]
    half = down.shape[1] // 2
    for x in range(SIDE):
        a = rows_a[x][...]
        b = jnp.concatenate(
            [rows_b[z][x].astype(F32) for z in range(SIDE)], axis=0
        ).astype(BF)
        gate = dot_nt(a, gate_up[0, :, :half]) + dot_nt(b, gate_up[0, :, half:])
        up = dot_nt(a, gate_up[1, :, :half]) + dot_nt(b, gate_up[1, :, half:])
        hidden[x] = (gate / (1.0 + jnp.exp(-gate)) * up).reshape(SIDE, ROWS, -1)
    for d in range(SIDE):
        part = hidden[d].reshape(SIDE * ROWS, -1)
        outs[d][...] = dot(part.astype(BF), down[:, :half]).astype(BF)
        part = hidden[:, d].reshape(SIDE * ROWS, -1)
        outs[SIDE + d][...] = dot(part.astype(BF), down[:, half:]).astype(BF)


def shared_expert(rows_a, rows_b, gate_up, down):
    half = down.shape[1] // 2
    count, width = SIDE * SIDE * ROWS, down.shape[1]
    return pl.pallas_call(
        shared_kernel,
        out_shape=[jax.ShapeDtypeStruct((SIDE * ROWS, half), BF)] * (2 * SIDE),
        scratch_shapes=[pltpu.VMEM((SIDE, SIDE, ROWS, down.shape[0]), F32)],
        compiler_params=vmem(48),
        cost_estimate=pl.CostEstimate(
            flops=6 * count * width * down.shape[0],
            bytes_accessed=2 * (2 * count * width + 3 * width * down.shape[0]),
            transcendentals=count * down.shape[0],
        ),
        name="shared_expert",
    )(*[a.reshape(SIDE * ROWS, half) for a in rows_a], *rows_b, gate_up, down)


def on_device(
    residual,
    prefill_qkv,
    decode_qkv,
    cache_pool,
    page_table,
    cache_len,
    out_weight,
    norm_gain,
    shared_gate_up,
    shared_down,
    shared_gate,
    routes,
    route_weight,
    expert_gate_up,
    expert_down,
):
    mine = lax.axis_index("exp")
    groups = lax.axis_size("exp")
    tok_rows, width = residual.shape
    devices = groups * lax.axis_size("req")
    experts_all = devices // 2
    route_count = routes.shape[1]
    capacity = 8

    flat = routes.reshape(-1)
    place = jnp.arange(flat.shape[0], dtype=jnp.int32)
    same = (flat[:, None] == flat[None, :]) & (place[None, :] < place[:, None])
    rank = jnp.sum(same.astype(jnp.int32), axis=1)
    slot_of = (flat * capacity + rank).reshape(tok_rows, route_count)
    slot_of = jnp.pad(slot_of, ((0, ROWS - tok_rows), (0, 0)), constant_values=-1)
    weight = jnp.pad(route_weight, ((0, ROWS - tok_rows), (0, 0)))
    tags = jnp.pad(
        routes.T.astype(F32),
        ((tok_rows, ROWS - tok_rows - route_count), (0, LANES - tok_rows)),
        constant_values=-1.0,
    )
    columns = jnp.arange(devices * capacity, dtype=jnp.int32)
    columns = columns // (2 * capacity) * capacity + columns % capacity
    mix = jnp.sum(
        jnp.where(slot_of[:, :, None] == columns[None, None, :], weight[:, :, None], 0.0), axis=1
    )
    mix_high = mix.astype(BF)
    mix_low = (mix - mix_high.astype(F32)).astype(BF)
    mix = jnp.concatenate([mix_high, mix_low], axis=0)

    attended = attention(prefill_qkv, decode_qkv, cache_pool, page_table, cache_len)
    sums = sum_first(project(attended, out_weight, mine[None]))
    got_a, got_b = sum_second(*lax.optimization_barrier(sums))
    stream, normed = pl.pallas_call(
        token_kernel,
        out_shape=[jax.ShapeDtypeStruct((ROWS, width), BF)] * 2,
        compiler_params=vmem(32),
        name="token_rows",
    )(
        *got_a,
        *got_b,
        jnp.pad(residual, ((0, ROWS - tok_rows), (0, 0))),
        norm_gain[None, :],
        tags,
    )
    rows_a, rows_b = gather(normed)
    outgoing = pick(mine[None], rows_a, rows_b, lax.axis_size("req"), capacity)
    arrived = lax.all_to_all(
        outgoing.reshape(lax.axis_size("req"), groups * capacity, width),
        "req",
        split_axis=0,
        concat_axis=0,
        tiled=True,
    )
    sums = sum_first(shared_expert(rows_a, rows_b, shared_gate_up.transpose(0, 2, 1), shared_down))
    got_a, got_b = sum_second(*lax.optimization_barrier(sums))
    arrived, got_a, got_b = lax.optimization_barrier((arrived, got_a, got_b))
    answer = experts(arrived.reshape(devices * capacity, width), expert_gate_up.transpose(0, 1, 3, 2), expert_down)
    returned = lax.all_to_all(
        answer.reshape(devices, capacity, width),
        ("req", "exp"),
        split_axis=0,
        concat_axis=0,
        tiled=True,
    )
    shared = jnp.concatenate([add_up(got_a), add_up(got_b)], axis=1)
    shared_scale = jax.nn.sigmoid(dot(normed, shared_gate))
    routed = dot(mix, returned.reshape(devices * capacity, width))
    routed = routed[:ROWS] + routed[ROWS:]
    result = stream.astype(F32) + routed + shared_scale[:, None] * shared
    return result[:tok_rows].astype(BF)


def solution(mesh):
    placed = (
        P(("req", "exp"), None),
        P("req", None, None, "exp"),
        P("req", None, "exp"),
        P(None, "req", None, "exp"),
        P("req", None),
        P("req"),
        P("exp", None),
        P(),
        P(None, None, "exp"),
        P("exp", None),
        P(),
        P(("req", "exp"), None),
        P(("req", "exp"), None),
        P(("req", "exp"), None, None, None),
        P(("req", "exp"), None, None),
    )
    return jax.shard_map(
        on_device, mesh=mesh, in_specs=placed, out_specs=P(("req", "exp"), None), check_vma=False
    )
```

```python
import functools

import jax
import jax.numpy as jnp
from jax import lax
from jax.experimental import pallas as pl
from jax.experimental.pallas import tpu as pltpu
from jax.sharding import PartitionSpec as P

HD = 128
SIDE = 4
TOKENS = 65
ROWS = 72
LANES = 128
ROUTES = 4
NEG_FILL = -1e30
MIB = 1 << 20
BF = jnp.bfloat16
F32 = jnp.float32
NT = (((1,), (1,)), ((), ()))


def vmem(limit):
    return pltpu.CompilerParams(vmem_limit_bytes=limit * MIB)


def dot(a, b):
    return jnp.dot(a, b, preferred_element_type=F32)


def dot_nt(a, b):
    return lax.dot_general(a, b, NT, preferred_element_type=F32)


def attention_kernel(lens, table, pre, dec, pool, out, keys, values, scores, sems):
    scale = HD ** (-0.5)
    copies = [
        pltpu.make_async_copy(pool.at[i], buf, sems.at[i]) for i, buf in enumerate((keys, values))
    ]
    for c in copies:
        c.start()
    spans, _, span, _ = pre.shape
    part = span // 2
    for r in range(spans):
        for h in range(2):
            width = part * (h + 1)
            q = pre[r, 0, h * part : (h + 1) * part, :]
            k = pre[r, 1, :width, :]
            v = pre[r, 2, :width, :]
            s = lax.dot_general(q, k, NT, preferred_element_type=F32) * scale
            row = lax.broadcasted_iota(jnp.int32, s.shape, 0) + h * part
            col = lax.broadcasted_iota(jnp.int32, s.shape, 1)
            s = jnp.where(col <= row, s, NEG_FILL)
            p = jnp.exp(s - jnp.max(s, axis=-1, keepdims=True))
            w = (p / jnp.sum(p, axis=-1, keepdims=True)).astype(BF)
            out[r * span + h * part : r * span + (h + 1) * part, :] = dot(w, v).astype(BF)
    requests, entries = table.shape
    pages, page = keys.shape[0], keys.shape[1]
    row = lax.broadcasted_iota(jnp.int32, (requests, entries), 0)
    held = jnp.zeros((requests, entries), jnp.int32)
    for i in range(requests):
        held = jnp.where(row == i, lens[i], held)
    held = jnp.clip(
        held - page * lax.broadcasted_iota(jnp.int32, (requests, entries), 1), 0, page
    )
    ids = table[...]
    lane = lax.broadcasted_iota(jnp.int32, (requests, page), 1)
    limit = jnp.zeros((requests, page), jnp.int32)
    for j in range(entries):
        limit = limit + jnp.where(ids[:, j : j + 1] == lane, held[:, j : j + 1], 0)
    q = dec[0]
    own = jnp.sum(q.astype(F32) * dec[1].astype(F32), axis=-1, keepdims=True) * scale
    group = 4
    wide = group * page
    copies[0].wait()
    top = jnp.full((requests, wide), NEG_FILL, F32)
    for c in range(pages // group):
        k = keys[c * group : (c + 1) * group].reshape(wide, HD)
        s = lax.dot_general(q, k, NT, preferred_element_type=F32) * scale
        s = jnp.concatenate(
            [
                jnp.where(
                    lane < limit[:, c * group + g : c * group + g + 1],
                    s[:, g * page : (g + 1) * page],
                    NEG_FILL,
                )
                for g in range(group)
            ],
            axis=1,
        )
        scores[:, c * wide : (c + 1) * wide] = s
        top = jnp.maximum(top, s)
    top = jnp.maximum(jnp.max(top, axis=-1, keepdims=True), own)
    total = jnp.zeros((requests, wide), F32)
    for c in range(pages // group):
        p = jnp.exp(scores[:, c * wide : (c + 1) * wide] - top)
        scores[:, c * wide : (c + 1) * wide] = p
        total = total + p
    own = jnp.exp(own - top)
    total = jnp.sum(total, axis=-1, keepdims=True) + own
    copies[1].wait()
    mixed = (own / total).astype(BF).astype(F32) * dec[2].astype(F32)
    for c in range(pages // group):
        w = (scores[:, c * wide : (c + 1) * wide] / total).astype(BF)
        mixed = mixed + dot(w, values[c * group : (c + 1) * group].reshape(wide, HD))
    out[spans * span : spans * span + requests, :] = mixed.astype(BF)


def attention(prefill_qkv, decode_qkv, cache_pool, page_table, cache_len):
    requests = decode_qkv.shape[0]
    pages, page = cache_pool.shape[1:3]
    rows = prefill_qkv.shape[0] * prefill_qkv.shape[2] + requests
    whole = pl.BlockSpec(memory_space=pltpu.VMEM)
    return pl.pallas_call(
        attention_kernel,
        out_shape=jax.ShapeDtypeStruct((rows, HD), BF),
        in_specs=[pl.BlockSpec(memory_space=pltpu.SMEM), whole, whole, whole, pl.BlockSpec(memory_space=pl.ANY)],
        out_specs=whole,
        scratch_shapes=[
            pltpu.VMEM((pages, page, HD), BF),
            pltpu.VMEM((pages, page, HD), BF),
            pltpu.VMEM((requests, pages * page), F32),
            pltpu.SemaphoreType.DMA((2,)),
        ],
        compiler_params=vmem(56),
        name="attention",
    )(cache_len, page_table, prefill_qkv, decode_qkv.transpose(1, 0, 2), cache_pool)


def project_kernel(mine, blocks, weight, *outs):
    half = weight.shape[1] // 2
    at_x, at_z = mine[0] // SIDE, mine[0] % SIDE

    def rows(picked):
        return jnp.concatenate([blocks[i].astype(F32) for i in picked], axis=0).astype(BF)

    xs = [jnp.bitwise_xor(at_x, d) * SIDE for d in range(SIDE)]
    zs = [jnp.bitwise_xor(at_z, d) for d in range(SIDE)]
    for d in range(SIDE):
        outs[d][...] = dot(rows([xs[d] + z for z in zs]), weight[:, :half]).astype(BF)
        outs[SIDE + d][...] = dot(rows([x + zs[d] for x in xs]), weight[:, half:]).astype(BF)


def project(attended, out_weight, mine):
    blocks = attended.reshape(SIDE * SIDE, -1, HD)
    blocks = jnp.pad(blocks, ((0, 0), (0, ROWS - blocks.shape[1]), (0, 0)))
    half = out_weight.shape[1] // 2
    whole = pl.BlockSpec(memory_space=pltpu.VMEM)
    return pl.pallas_call(
        project_kernel,
        out_shape=[jax.ShapeDtypeStruct((SIDE * ROWS, half), BF)] * (2 * SIDE),
        in_specs=[pl.BlockSpec(memory_space=pltpu.SMEM), whole, whole],
        out_specs=[whole] * (2 * SIDE),
        compiler_params=vmem(56),
        name="project",
    )(mine, blocks, out_weight)


def along_x(a, d):
    return lax.ppermute(a, "exp", [(i, i ^ (d * SIDE)) for i in range(SIDE * SIDE)])


def along_z(a, d):
    return lax.ppermute(a, "exp", [(i, i ^ d) for i in range(SIDE * SIDE)])


def add_up(parts):
    total = parts[0].astype(F32)
    for p in parts[1:]:
        total = total + p.astype(F32)
    return total


def sum_first(parts):
    parts_a, parts_b = parts[:SIDE], parts[SIDE:]
    got_a, got_b = [parts_a[0]], [parts_b[0]]
    for d in (1, 3, 2):
        got_a.append(along_x(parts_a[d], d))
        got_b.append(along_z(parts_b[d], d))
    sum_a = add_up(got_a).astype(BF).reshape(SIDE, ROWS, -1)
    sum_b = add_up(got_b).astype(BF).reshape(SIDE, ROWS, -1)
    return sum_a, sum_b


def sum_second(sum_a, sum_b):
    got_a, got_b = [sum_a[0]], [sum_b[0]]
    for d in (1, 3, 2):
        got_a.append(along_z(sum_a[d], d))
        got_b.append(along_x(sum_b[d], d))
    return got_a, got_b


def gather(rows):
    half = rows.shape[1] // 2
    rows_a, rows_b = rows[:, :half], rows[:, half:]
    got_a, got_b = {0: rows_a}, {0: rows_b}
    for d in (1, 3, 2):
        got_a[d] = along_z(rows_a, d)
        got_b[d] = along_x(rows_b, d)
    rows_a = jnp.stack([got_a[d] for d in range(SIDE)])
    rows_b = jnp.stack([got_b[d] for d in range(SIDE)])
    rows_a, rows_b = lax.optimization_barrier((rows_a, rows_b))
    got_a, got_b = {0: rows_a}, {0: rows_b}
    for d in (1, 3, 2):
        got_a[d] = along_x(rows_a, d)
        got_b[d] = along_z(rows_b, d)
    return [got_a[d] for d in range(SIDE)], [got_b[d] for d in range(SIDE)]


def token_kernel(a0, a1, a2, a3, b0, b1, b2, b3, residual, gain, tags, stream, normed):
    f = lambda r: r[...].astype(F32)
    projected = jnp.concatenate(
        [f(a0) + f(a1) + f(a2) + f(a3), f(b0) + f(b1) + f(b2) + f(b3)], axis=1
    )
    held = (f(residual) + projected).astype(BF)
    stream[...] = held
    wide = held.astype(F32)
    mean = jnp.mean(wide * wide, axis=-1, keepdims=True)
    rows = wide * lax.rsqrt(mean + 1e-06) * gain[...]
    normed[...] = rows.astype(BF)
    count, lanes = tags.shape
    is_tag = lax.broadcasted_iota(jnp.int32, (count, lanes), 0) >= TOKENS
    for at in (0, rows.shape[1] // 2):
        normed[:, at : at + lanes] = jnp.where(is_tag, tags[...], rows[:, at : at + lanes]).astype(BF)


def chosen_rows(mine, tags, columns, capacity):
    shape = (columns, LANES)
    expert = lax.broadcasted_iota(jnp.int32, shape, 0) * (SIDE * SIDE // 2) + mine // 2
    expert = expert.astype(F32)
    hits = []
    for block in tags:
        wide = block.astype(F32)
        hit = jnp.zeros(shape, F32)
        for k in range(ROUTES):
            named = jnp.broadcast_to(wide[TOKENS + k : TOKENS + k + 1, :], shape)
            hit = jnp.where(named == expert, 1.0, hit)
        hits.append(hit)
    hits = jnp.concatenate(hits, axis=0)
    before = lax.broadcasted_iota(jnp.int32, (LANES, LANES), 0) < lax.broadcasted_iota(
        jnp.int32, (LANES, LANES), 1
    )
    rank = dot(hits.astype(BF), before.astype(F32).astype(BF))
    rank = jnp.where(hits > 0.0, rank, -1.0)
    slot = lax.broadcasted_iota(jnp.int32, (columns, capacity, LANES), 1).astype(F32)
    chosen = []
    for i in range(len(tags)):
        here = rank[i * columns : (i + 1) * columns, :]
        here = jnp.broadcast_to(here[:, None, :], (columns, capacity, LANES))
        here = jnp.where(here == slot, 1.0, 0.0).reshape(columns * capacity, LANES)
        chosen.append(here[:, :ROWS].astype(BF))
    return chosen


def pick_kernel(start, mine, *refs):
    rows_a, rows_b, out = refs[:2], refs[2:4], refs[4]
    columns, _, _, capacity, _ = out.shape
    own = range(start, start + 2)
    pairs = [(x, z) for x in range(SIDE) for z in range(SIDE) if x in own or z in own]
    tags = [
        rows_a[x - start][z][:, :LANES] if x in own else rows_b[z - start][x][:, :LANES]
        for x, z in pairs
    ]
    for (x, z), pick in zip(pairs, chosen_rows(mine[0], tags, columns, capacity)):
        if x in own:
            a = dot(pick, rows_a[x - start][z]).reshape(columns, capacity, -1).astype(BF)
            for r in range(columns):
                out[r, 0, (x - start) * SIDE + z] = a[r]
        if z in own:
            b = dot(pick, rows_b[z - start][x]).reshape(columns, capacity, -1).astype(BF)
            for r in range(columns):
                out[r, 1, x * 2 + z - start] = b[r]


def pick(start, mine, rows, columns, capacity):
    whole = pl.BlockSpec(memory_space=pltpu.VMEM)
    half = rows[0].shape[-1]
    return pl.pallas_call(
        functools.partial(pick_kernel, start),
        out_shape=jax.ShapeDtypeStruct((columns, 2, 2 * SIDE, capacity, half), BF),
        in_specs=[pl.BlockSpec(memory_space=pltpu.SMEM)] + [whole] * 4,
        out_specs=whole,
        compiler_params=vmem(56),
        name="pick",
    )(mine, *rows)


def expert_kernel(mine, first, second, gate_up, down, out):
    step, _, height, half = first.shape
    piece = height // SIDE
    a, b = [], []
    for i in range(step):
        a += [first[i, 0], second[i, 0]]
        for x in range(SIDE):
            b += [first[i, 1, x * piece : (x + 1) * piece], second[i, 1, x * piece : (x + 1) * piece]]
    a = jnp.concatenate(a, axis=0)
    b = jnp.concatenate(b, axis=0)
    gate = dot_nt(a, gate_up[0, 0, :, :half]) + dot_nt(b, gate_up[0, 0, :, half:])
    up = dot_nt(a, gate_up[0, 1, :, :half]) + dot_nt(b, gate_up[0, 1, :, half:])
    hidden = (gate / (1.0 + jnp.exp(-gate)) * up).astype(BF)
    _, blocks, capacity, width = out.shape
    answer = dot(hidden, down[0]).reshape(step, blocks, capacity, width)
    for i in range(step):
        for d in range(blocks):
            out[i, jnp.bitwise_xor(mine[0], d)] = answer[i, d].astype(BF)


def experts(mine, first, second, gate_up, down, capacity):
    count, _, height, half = first.shape
    step = 4
    width = 2 * half
    blocks = 2 * height // capacity
    rows = count * blocks * capacity
    tile = pl.BlockSpec((step, 2, height, half), lambda i: (i, 0, 0, 0))
    return pl.pallas_call(
        expert_kernel,
        grid=(count // step,),
        out_shape=jax.ShapeDtypeStruct((count, blocks, capacity, width), BF),
        in_specs=[
            pl.BlockSpec(memory_space=pltpu.SMEM),
            tile,
            tile,
            pl.BlockSpec(gate_up.shape, lambda i: (0, 0, 0, 0)),
            pl.BlockSpec(down.shape, lambda i: (0, 0, 0)),
        ],
        out_specs=pl.BlockSpec((step, blocks, capacity, width), lambda i: (i, 0, 0, 0)),
        compiler_params=vmem(50),
        cost_estimate=pl.CostEstimate(
            flops=6 * rows * width * down.shape[1],
            bytes_accessed=2 * (2 * rows * width + 3 * width * down.shape[1]),
            transcendentals=rows * down.shape[1],
        ),
        name="experts",
    )(mine, first, second, gate_up, down)


def shared_kernel(*refs):
    rows_a, rows_b = refs[:SIDE], refs[SIDE : 2 * SIDE]
    gate_up, down = refs[2 * SIDE : 2 * SIDE + 2]
    outs, hidden = refs[2 * SIDE + 2 : -1], refs[-1]
    half = down.shape[1] // 2
    for x in range(SIDE):
        a = rows_a[x][...]
        b = jnp.concatenate(
            [rows_b[z][x].astype(F32) for z in range(SIDE)], axis=0
        ).astype(BF)
        gate = dot_nt(a, gate_up[0, :, :half]) + dot_nt(b, gate_up[0, :, half:])
        up = dot_nt(a, gate_up[1, :, :half]) + dot_nt(b, gate_up[1, :, half:])
        hidden[x] = (gate / (1.0 + jnp.exp(-gate)) * up).reshape(SIDE, ROWS, -1)
    for d in range(SIDE):
        part = hidden[d].reshape(SIDE * ROWS, -1)
        outs[d][...] = dot(part.astype(BF), down[:, :half]).astype(BF)
        part = hidden[:, d].reshape(SIDE * ROWS, -1)
        outs[SIDE + d][...] = dot(part.astype(BF), down[:, half:]).astype(BF)


def shared_expert(rows_a, rows_b, gate_up, down):
    half = down.shape[1] // 2
    count, width = SIDE * SIDE * ROWS, down.shape[1]
    return pl.pallas_call(
        shared_kernel,
        out_shape=[jax.ShapeDtypeStruct((SIDE * ROWS, half), BF)] * (2 * SIDE),
        scratch_shapes=[pltpu.VMEM((SIDE, SIDE, ROWS, down.shape[0]), F32)],
        compiler_params=vmem(48),
        cost_estimate=pl.CostEstimate(
            flops=6 * count * width * down.shape[0],
            bytes_accessed=2 * (2 * count * width + 3 * width * down.shape[0]),
            transcendentals=count * down.shape[0],
        ),
        name="shared_expert",
    )(*[a.reshape(SIDE * ROWS, half) for a in rows_a], *rows_b, gate_up, down)


def on_device(
    residual,
    prefill_qkv,
    decode_qkv,
    cache_pool,
    page_table,
    cache_len,
    out_weight,
    norm_gain,
    shared_gate_up,
    shared_down,
    shared_gate,
    routes,
    route_weight,
    expert_gate_up,
    expert_down,
):
    mine = lax.axis_index("exp")
    groups = lax.axis_size("exp")
    tok_rows, width = residual.shape
    devices = groups * lax.axis_size("req")
    experts_all = devices // 2
    route_count = routes.shape[1]
    capacity = 8

    flat = routes.reshape(-1)
    place = jnp.arange(flat.shape[0], dtype=jnp.int32)
    same = (flat[:, None] == flat[None, :]) & (place[None, :] < place[:, None])
    rank = jnp.sum(same.astype(jnp.int32), axis=1)
    slot_of = (flat * capacity + rank).reshape(tok_rows, route_count)
    slot_of = jnp.pad(slot_of, ((0, ROWS - tok_rows), (0, 0)), constant_values=-1)
    weight = jnp.pad(route_weight, ((0, ROWS - tok_rows), (0, 0)))
    tags = jnp.pad(
        routes.T.astype(F32),
        ((tok_rows, ROWS - tok_rows - route_count), (0, LANES - tok_rows)),
        constant_values=-1.0,
    )
    columns = jnp.arange(devices * capacity, dtype=jnp.int32)
    columns = columns // (2 * capacity) * capacity + columns % capacity
    mix = jnp.sum(
        jnp.where(slot_of[:, :, None] == columns[None, None, :], weight[:, :, None], 0.0), axis=1
    )
    mix_high = mix.astype(BF)
    mix_low = (mix - mix_high.astype(F32)).astype(BF)
    mix = jnp.concatenate([mix_high, mix_low], axis=0)

    attended = attention(prefill_qkv, decode_qkv, cache_pool, page_table, cache_len)
    sums = sum_first(project(attended, out_weight, mine[None]))
    got_a, got_b = sum_second(*lax.optimization_barrier(sums))
    stream, normed = pl.pallas_call(
        token_kernel,
        out_shape=[jax.ShapeDtypeStruct((ROWS, width), BF)] * 2,
        compiler_params=vmem(32),
        name="token_rows",
    )(
        *got_a,
        *got_b,
        jnp.pad(residual, ((0, ROWS - tok_rows), (0, 0))),
        norm_gain[None, :],
        tags,
    )
    rows_a, rows_b = gather(normed)
    req = lax.axis_size("req")

    def exchange(picked):
        picked = picked.reshape(req, groups * capacity, width // 2)
        picked = lax.all_to_all(picked, "req", split_axis=0, concat_axis=0, tiled=True)
        return picked.reshape(req, 2, -1, width // 2)

    first = pick(0, mine[None], [*rows_a[:2], *rows_b[:2]], req, capacity)
    first, *late = lax.optimization_barrier((first, *rows_a[2:], *rows_b[2:]))
    first = exchange(first)
    second = exchange(pick(2, mine[None], late, req, capacity))
    rows_a, rows_b = [*rows_a[:2], *late[:2]], [*rows_b[:2], *late[2:]]
    sums = sum_first(shared_expert(rows_a, rows_b, shared_gate_up.transpose(0, 2, 1), shared_down))
    answer = experts(
        mine[None], first, second, expert_gate_up.transpose(0, 1, 3, 2), expert_down, capacity
    )
    answer, *sums = lax.optimization_barrier((answer, *sums))
    returned = lax.all_to_all(
        answer.reshape(devices, capacity, width),
        ("req", "exp"),
        split_axis=0,
        concat_axis=0,
        tiled=True,
    )
    got_a, got_b = sum_second(*sums)
    shared = jnp.concatenate([add_up(got_a), add_up(got_b)], axis=1)
    shared_scale = jax.nn.sigmoid(dot(normed, shared_gate))
    routed = dot(mix, returned.reshape(devices * capacity, width))
    routed = routed[:ROWS] + routed[ROWS:]
    result = stream.astype(F32) + routed + shared_scale[:, None] * shared
    return result[:tok_rows].astype(BF)


def solution(mesh):
    placed = (
        P(("req", "exp"), None),
        P("req", None, None, "exp"),
        P("req", None, "exp"),
        P(None, "req", None, "exp"),
        P("req", None),
        P("req"),
        P("exp", None),
        P(),
        P(None, None, "exp"),
        P("exp", None),
        P(),
        P(("req", "exp"), None),
        P(("req", "exp"), None),
        P(("req", "exp"), None, None, None),
        P(("req", "exp"), None, None),
    )
    return jax.shard_map(
        on_device, mesh=mesh, in_specs=placed, out_specs=P(("req", "exp"), None), check_vma=False
    )
```

```python
import functools

import jax
import jax.numpy as jnp
from jax import lax
from jax.experimental import pallas as pl
from jax.experimental.pallas import tpu as pltpu
from jax.sharding import PartitionSpec as P

HD = 128
SIDE = 4
TOKENS = 65
ROWS = 72
LANES = 128
ROUTES = 4
PIECES = 5
NEG_FILL = -1e30
MIB = 1 << 20
BF = jnp.bfloat16
F32 = jnp.float32
NT = (((1,), (1,)), ((), ()))


def vmem(limit):
    return pltpu.CompilerParams(vmem_limit_bytes=limit * MIB)


def dot(a, b):
    return jnp.dot(a, b, preferred_element_type=F32)


def dot_nt(a, b):
    return lax.dot_general(a, b, NT, preferred_element_type=F32)


def attention_kernel(lens, table, pre, dec, pool, out, keys, values, scores, sems):
    scale = HD ** (-0.5)
    copies = [
        pltpu.make_async_copy(pool.at[i], buf, sems.at[i]) for i, buf in enumerate((keys, values))
    ]
    for c in copies:
        c.start()
    spans, _, span, _ = pre.shape
    part = span // 2
    for r in range(spans):
        for h in range(2):
            width = part * (h + 1)
            q = pre[r, 0, h * part : (h + 1) * part, :]
            k = pre[r, 1, :width, :]
            v = pre[r, 2, :width, :]
            s = lax.dot_general(q, k, NT, preferred_element_type=F32) * scale
            row = lax.broadcasted_iota(jnp.int32, s.shape, 0) + h * part
            col = lax.broadcasted_iota(jnp.int32, s.shape, 1)
            s = jnp.where(col <= row, s, NEG_FILL)
            p = jnp.exp(s - jnp.max(s, axis=-1, keepdims=True))
            w = (p / jnp.sum(p, axis=-1, keepdims=True)).astype(BF)
            out[r * span + h * part : r * span + (h + 1) * part, :] = dot(w, v).astype(BF)
    requests, entries = table.shape
    pages, page = keys.shape[0], keys.shape[1]
    row = lax.broadcasted_iota(jnp.int32, (requests, entries), 0)
    held = jnp.zeros((requests, entries), jnp.int32)
    for i in range(requests):
        held = jnp.where(row == i, lens[i], held)
    held = jnp.clip(
        held - page * lax.broadcasted_iota(jnp.int32, (requests, entries), 1), 0, page
    )
    ids = table[...]
    lane = lax.broadcasted_iota(jnp.int32, (requests, page), 1)
    limit = jnp.zeros((requests, page), jnp.int32)
    for j in range(entries):
        limit = limit + jnp.where(ids[:, j : j + 1] == lane, held[:, j : j + 1], 0)
    q = dec[0]
    own = jnp.sum(q.astype(F32) * dec[1].astype(F32), axis=-1, keepdims=True) * scale
    group = 4
    wide = group * page
    copies[0].wait()
    top = jnp.full((requests, wide), NEG_FILL, F32)
    for c in range(pages // group):
        k = keys[c * group : (c + 1) * group].reshape(wide, HD)
        s = lax.dot_general(q, k, NT, preferred_element_type=F32) * scale
        s = jnp.concatenate(
            [
                jnp.where(
                    lane < limit[:, c * group + g : c * group + g + 1],
                    s[:, g * page : (g + 1) * page],
                    NEG_FILL,
                )
                for g in range(group)
            ],
            axis=1,
        )
        scores[:, c * wide : (c + 1) * wide] = s
        top = jnp.maximum(top, s)
    top = jnp.maximum(jnp.max(top, axis=-1, keepdims=True), own)
    total = jnp.zeros((requests, wide), F32)
    for c in range(pages // group):
        p = jnp.exp(scores[:, c * wide : (c + 1) * wide] - top)
        scores[:, c * wide : (c + 1) * wide] = p
        total = total + p
    own = jnp.exp(own - top)
    total = jnp.sum(total, axis=-1, keepdims=True) + own
    copies[1].wait()
    mixed = (own / total).astype(BF).astype(F32) * dec[2].astype(F32)
    for c in range(pages // group):
        w = (scores[:, c * wide : (c + 1) * wide] / total).astype(BF)
        mixed = mixed + dot(w, values[c * group : (c + 1) * group].reshape(wide, HD))
    out[spans * span : spans * span + requests, :] = mixed.astype(BF)


def attention(prefill_qkv, decode_qkv, cache_pool, page_table, cache_len):
    requests = decode_qkv.shape[0]
    pages, page = cache_pool.shape[1:3]
    rows = prefill_qkv.shape[0] * prefill_qkv.shape[2] + requests
    whole = pl.BlockSpec(memory_space=pltpu.VMEM)
    return pl.pallas_call(
        attention_kernel,
        out_shape=jax.ShapeDtypeStruct((rows, HD), BF),
        in_specs=[pl.BlockSpec(memory_space=pltpu.SMEM), whole, whole, whole, pl.BlockSpec(memory_space=pl.ANY)],
        out_specs=whole,
        scratch_shapes=[
            pltpu.VMEM((pages, page, HD), BF),
            pltpu.VMEM((pages, page, HD), BF),
            pltpu.VMEM((requests, pages * page), F32),
            pltpu.SemaphoreType.DMA((2,)),
        ],
        compiler_params=vmem(48),
        name="attention",
    )(cache_len, page_table, prefill_qkv, decode_qkv.transpose(1, 0, 2), cache_pool)


def project_kernel(mine, blocks, weight, *outs):
    half = weight.shape[1] // 2
    at_x, at_z = mine[0] // SIDE, mine[0] % SIDE

    def rows(picked):
        return jnp.concatenate([blocks[i].astype(F32) for i in picked], axis=0).astype(BF)

    xs = [jnp.bitwise_xor(at_x, d) * SIDE for d in range(SIDE)]
    zs = [jnp.bitwise_xor(at_z, d) for d in range(SIDE)]
    for d in range(SIDE):
        outs[d][...] = dot(rows([xs[d] + z for z in zs]), weight[:, :half]).astype(BF)
        outs[SIDE + d][...] = dot(rows([x + zs[d] for x in xs]), weight[:, half:]).astype(BF)


def project(attended, out_weight, mine):
    blocks = attended.reshape(SIDE * SIDE, -1, HD)
    blocks = jnp.pad(blocks, ((0, 0), (0, ROWS - blocks.shape[1]), (0, 0)))
    half = out_weight.shape[1] // 2
    whole = pl.BlockSpec(memory_space=pltpu.VMEM)
    return pl.pallas_call(
        project_kernel,
        out_shape=[jax.ShapeDtypeStruct((SIDE * ROWS, half), BF)] * (2 * SIDE),
        in_specs=[pl.BlockSpec(memory_space=pltpu.SMEM), whole, whole],
        out_specs=[whole] * (2 * SIDE),
        compiler_params=vmem(32),
        name="project",
    )(mine, blocks, out_weight)


def along_x(a, d):
    return lax.ppermute(a, "exp", [(i, i ^ (d * SIDE)) for i in range(SIDE * SIDE)])


def along_z(a, d):
    return lax.ppermute(a, "exp", [(i, i ^ d) for i in range(SIDE * SIDE)])


def add_up(parts):
    total = parts[0].astype(F32)
    for p in parts[1:]:
        total = total + p.astype(F32)
    return total


def ring_sum(parts, along):
    half = parts[0].shape[0] // 2
    near = along(parts[2][:half], 1)
    far = along(parts[2][half:], 3)
    one = jnp.concatenate([parts[1][:half], add_up([parts[1][half:], far]).astype(BF)], axis=0)
    three = jnp.concatenate([add_up([parts[3][:half], near]).astype(BF), parts[3][half:]], axis=0)
    return one, three


def sum_first(parts):
    parts_a, parts_b = parts[:SIDE], parts[SIDE:]
    one_a, three_a = ring_sum(parts_a, along_x)
    one_b, three_b = ring_sum(parts_b, along_z)
    one_a, three_a, one_b, three_b = lax.optimization_barrier((one_a, three_a, one_b, three_b))
    got_a = [parts_a[0], along_x(one_a, 1), along_x(three_a, 3)]
    got_b = [parts_b[0], along_z(one_b, 1), along_z(three_b, 3)]
    sum_a = add_up(got_a).astype(BF).reshape(SIDE, ROWS, -1)
    sum_b = add_up(got_b).astype(BF).reshape(SIDE, ROWS, -1)
    return sum_a, sum_b


def sum_second(sum_a, sum_b):
    got_a, got_b = [sum_a[0]], [sum_b[0]]
    for d in (1, 3, 2):
        got_a.append(along_z(sum_a[d], d))
        got_b.append(along_x(sum_b[d], d))
    return got_a, got_b


def gather(rows):
    half = rows.shape[1] // 2
    rows_a, rows_b = rows[:, :half], rows[:, half:]
    got_a, got_b = {0: rows_a}, {0: rows_b}
    for d in (1, 3, 2):
        got_a[d] = along_z(rows_a, d)
        got_b[d] = along_x(rows_b, d)
    rows_a = jnp.stack([got_a[d] for d in range(SIDE)])
    rows_b = jnp.stack([got_b[d] for d in range(SIDE)])
    rows_a, rows_b = lax.optimization_barrier((rows_a, rows_b))
    one_a, one_b = along_x(rows_a, 1), along_z(rows_b, 1)
    three_a, three_b = along_x(rows_a, 3), along_z(rows_b, 3)
    half = SIDE // 2
    return (
        [rows_a, one_a, three_a, along_x(three_a[:half], 1), along_x(one_a[half:], 3)],
        [rows_b, one_b, three_b, along_z(three_b[:half], 1), along_z(one_b[half:], 3)],
    )


def block_of(pieces, d, i):
    if d == 2:
        return pieces[3][i] if i < SIDE // 2 else pieces[4][i - SIDE // 2]
    return pieces[{0: 0, 1: 1, 3: 2}[d]][i]


def token_kernel(a0, a1, a2, a3, b0, b1, b2, b3, residual, gain, tags, stream, normed):
    f = lambda r: r[...].astype(F32)
    projected = jnp.concatenate(
        [f(a0) + f(a1) + f(a2) + f(a3), f(b0) + f(b1) + f(b2) + f(b3)], axis=1
    )
    held = (f(residual) + projected).astype(BF)
    stream[...] = held
    wide = held.astype(F32)
    mean = jnp.mean(wide * wide, axis=-1, keepdims=True)
    rows = wide * lax.rsqrt(mean + 1e-06) * gain[...]
    normed[...] = rows.astype(BF)
    count, lanes = tags.shape
    is_tag = lax.broadcasted_iota(jnp.int32, (count, lanes), 0) >= TOKENS
    normed[:, :lanes] = jnp.where(is_tag, tags[...], rows[:, :lanes]).astype(BF)


def chosen_rows(mine, rows_a, columns, capacity):
    shape = (columns, LANES)
    expert = lax.broadcasted_iota(jnp.int32, shape, 0) * (SIDE * SIDE // 2) + mine // 2
    expert = expert.astype(F32)
    hits = []
    for x in range(SIDE):
        for z in range(SIDE):
            tags = block_of(rows_a, x, z)[:, :LANES].astype(F32)
            hit = jnp.zeros(shape, F32)
            for k in range(ROUTES):
                named = jnp.broadcast_to(tags[TOKENS + k : TOKENS + k + 1, :], shape)
                hit = jnp.where(named == expert, 1.0, hit)
            hits.append(hit)
    hits = jnp.concatenate(hits, axis=0)
    before = lax.broadcasted_iota(jnp.int32, (LANES, LANES), 0) < lax.broadcasted_iota(
        jnp.int32, (LANES, LANES), 1
    )
    rank = dot(hits.astype(BF), before.astype(F32).astype(BF))
    rank = jnp.where(hits > 0.0, rank, -1.0)
    slot = lax.broadcasted_iota(jnp.int32, (columns, capacity, LANES), 1).astype(F32)
    chosen = []
    for i in range(SIDE * SIDE):
        here = rank[i * columns : (i + 1) * columns, :]
        here = jnp.broadcast_to(here[:, None, :], (columns, capacity, LANES))
        here = jnp.where(here == slot, 1.0, 0.0).reshape(columns * capacity, LANES)
        chosen.append(here[:, :ROWS].astype(BF))
    return chosen


def pick_kernel(mine, *refs):
    rows_a, rows_b, out = refs[:PIECES], refs[PIECES : 2 * PIECES], refs[-1]
    columns, _, capacity, width = out.shape
    half = width // 2
    chosen = chosen_rows(mine[0], rows_a, columns, capacity)
    for x in range(SIDE):
        for z in range(SIDE):
            block = jnp.bitwise_xor(mine[0], x * SIDE + z)
            pick = chosen[x * SIDE + z]
            a = dot(pick, block_of(rows_a, x, z)).reshape(columns, capacity, half).astype(BF)
            b = dot(pick, block_of(rows_b, z, x)).reshape(columns, capacity, half).astype(BF)
            for r in range(columns):
                out[r, block, :, :half] = a[r]
                out[r, block, :, half:] = b[r]


def pick(mine, rows_a, rows_b, columns, capacity):
    width = 2 * rows_a[0].shape[-1]
    whole = pl.BlockSpec(memory_space=pltpu.VMEM)
    return pl.pallas_call(
        pick_kernel,
        out_shape=jax.ShapeDtypeStruct((columns, SIDE * SIDE, capacity, width), BF),
        in_specs=[pl.BlockSpec(memory_space=pltpu.SMEM)] + [whole] * (2 * PIECES),
        out_specs=whole,
        compiler_params=vmem(56),
        name="pick",
    )(mine, *rows_a, *rows_b)


def expert_kernel(rows, gate_up, down, out):
    x = rows[...]
    gate = dot_nt(x, gate_up[0, 0])
    up = dot_nt(x, gate_up[0, 1])
    hidden = (gate / (1.0 + jnp.exp(-gate)) * up).astype(BF)
    out[...] = dot(hidden, down[0]).astype(BF)


def experts(rows, gate_up, down):
    count, width = rows.shape
    step = 512
    return pl.pallas_call(
        expert_kernel,
        grid=(count // step,),
        out_shape=jax.ShapeDtypeStruct((count, width), BF),
        in_specs=[
            pl.BlockSpec((step, width), lambda i: (i, 0)),
            pl.BlockSpec(gate_up.shape, lambda i: (0, 0, 0, 0)),
            pl.BlockSpec(down.shape, lambda i: (0, 0, 0)),
        ],
        out_specs=pl.BlockSpec((step, width), lambda i: (i, 0)),
        compiler_params=vmem(56),
        cost_estimate=pl.CostEstimate(
            flops=6 * count * width * down.shape[1],
            bytes_accessed=2 * (2 * count * width + 3 * width * down.shape[1]),
            transcendentals=count * down.shape[1],
        ),
        name="experts",
    )(rows, gate_up, down)


def shared_kernel(*refs):
    rows_a, rows_b = refs[:PIECES], refs[PIECES : 2 * PIECES]
    gate_up, down = refs[2 * PIECES : 2 * PIECES + 2]
    outs, hidden = refs[2 * PIECES + 2 : -1], refs[-1]
    half = down.shape[1] // 2
    for x in range(SIDE):
        a, b = (
            jnp.concatenate(blocks, axis=0).astype(BF)
            for blocks in (
                [block_of(rows_a, x, z).astype(F32) for z in range(SIDE)],
                [block_of(rows_b, z, x).astype(F32) for z in range(SIDE)],
            )
        )
        gate = dot_nt(a, gate_up[0, :, :half]) + dot_nt(b, gate_up[0, :, half:])
        up = dot_nt(a, gate_up[1, :, :half]) + dot_nt(b, gate_up[1, :, half:])
        hidden[x] = (gate / (1.0 + jnp.exp(-gate)) * up).reshape(SIDE, ROWS, -1)
    for d in range(SIDE):
        part = hidden[d].reshape(SIDE * ROWS, -1)
        outs[d][...] = dot(part.astype(BF), down[:, :half]).astype(BF)
        part = hidden[:, d].reshape(SIDE * ROWS, -1)
        outs[SIDE + d][...] = dot(part.astype(BF), down[:, half:]).astype(BF)


def shared_expert(rows_a, rows_b, gate_up, down):
    half = down.shape[1] // 2
    count, width = SIDE * SIDE * ROWS, down.shape[1]
    return pl.pallas_call(
        shared_kernel,
        out_shape=[jax.ShapeDtypeStruct((SIDE * ROWS, half), BF)] * (2 * SIDE),
        scratch_shapes=[pltpu.VMEM((SIDE, SIDE, ROWS, down.shape[0]), F32)],
        compiler_params=vmem(48),
        cost_estimate=pl.CostEstimate(
            flops=6 * count * width * down.shape[0],
            bytes_accessed=2 * (2 * count * width + 3 * width * down.shape[0]),
            transcendentals=count * down.shape[0],
        ),
        name="shared_expert",
    )(*rows_a, *rows_b, gate_up, down)


def on_device(
    residual,
    prefill_qkv,
    decode_qkv,
    cache_pool,
    page_table,
    cache_len,
    out_weight,
    norm_gain,
    shared_gate_up,
    shared_down,
    shared_gate,
    routes,
    route_weight,
    expert_gate_up,
    expert_down,
):
    mine = lax.axis_index("exp")
    groups = lax.axis_size("exp")
    tok_rows, width = residual.shape
    devices = groups * lax.axis_size("req")
    experts_all = devices // 2
    route_count = routes.shape[1]
    capacity = 8

    flat = routes.reshape(-1)
    place = jnp.arange(flat.shape[0], dtype=jnp.int32)
    same = (flat[:, None] == flat[None, :]) & (place[None, :] < place[:, None])
    rank = jnp.sum(same.astype(jnp.int32), axis=1)
    slot_of = (flat * capacity + rank).reshape(tok_rows, route_count)
    slot_of = jnp.pad(slot_of, ((0, ROWS - tok_rows), (0, 0)), constant_values=-1)
    weight = jnp.pad(route_weight, ((0, ROWS - tok_rows), (0, 0)))
    tags = jnp.pad(
        routes.T.astype(F32),
        ((tok_rows, ROWS - tok_rows - route_count), (0, LANES - tok_rows)),
        constant_values=-1.0,
    )
    columns = jnp.arange(devices * capacity, dtype=jnp.int32)
    columns = columns // (2 * capacity) * capacity + columns % capacity
    mix = jnp.sum(
        jnp.where(slot_of[:, :, None] == columns[None, None, :], weight[:, :, None], 0.0), axis=1
    )
    mix_high = mix.astype(BF)
    mix_low = (mix - mix_high.astype(F32)).astype(BF)
    mix = jnp.concatenate([mix_high, mix_low], axis=0)

    attended = attention(prefill_qkv, decode_qkv, cache_pool, page_table, cache_len)
    sums = sum_first(project(attended, out_weight, mine[None]))
    got_a, got_b = sum_second(*lax.optimization_barrier(sums))
    stream, normed = pl.pallas_call(
        token_kernel,
        out_shape=[jax.ShapeDtypeStruct((ROWS, width), BF)] * 2,
        compiler_params=vmem(32),
        name="token_rows",
    )(
        *got_a,
        *got_b,
        jnp.pad(residual, ((0, ROWS - tok_rows), (0, 0))),
        norm_gain[None, :],
        tags,
    )
    rows_a, rows_b = gather(normed)
    outgoing = pick(mine[None], rows_a, rows_b, lax.axis_size("req"), capacity)
    arrived = lax.all_to_all(
        outgoing.reshape(lax.axis_size("req"), groups * capacity, width),
        "req",
        split_axis=0,
        concat_axis=0,
        tiled=True,
    )
    sums = sum_first(shared_expert(rows_a, rows_b, shared_gate_up.transpose(0, 2, 1), shared_down))
    got_a, got_b = sum_second(*lax.optimization_barrier(sums))
    arrived, got_a, got_b = lax.optimization_barrier((arrived, got_a, got_b))
    answer = experts(arrived.reshape(devices * capacity, width), expert_gate_up.transpose(0, 1, 3, 2), expert_down)
    returned = lax.all_to_all(
        answer.reshape(devices, capacity, width),
        ("req", "exp"),
        split_axis=0,
        concat_axis=0,
        tiled=True,
    )
    shared = jnp.concatenate([add_up(got_a), add_up(got_b)], axis=1)
    shared_scale = jax.nn.sigmoid(dot(normed, shared_gate))
    routed = dot(mix, returned.reshape(devices * capacity, width))
    routed = routed[:ROWS] + routed[ROWS:]
    result = stream.astype(F32) + routed + shared_scale[:, None] * shared
    return result[:tok_rows].astype(BF)


def solution(mesh):
    placed = (
        P(("req", "exp"), None),
        P("req", None, None, "exp"),
        P("req", None, "exp"),
        P(None, "req", None, "exp"),
        P("req", None),
        P("req"),
        P("exp", None),
        P(),
        P(None, None, "exp"),
        P("exp", None),
        P(),
        P(("req", "exp"), None),
        P(("req", "exp"), None),
        P(("req", "exp"), None, None, None),
        P(("req", "exp"), None, None),
    )
    return jax.shard_map(
        on_device, mesh=mesh, in_specs=placed, out_specs=P(("req", "exp"), None), check_vma=False
    )
```

```python
import functools

import jax
import jax.numpy as jnp
from jax import lax
from jax.experimental import pallas as pl
from jax.experimental.pallas import tpu as pltpu
from jax.sharding import PartitionSpec as P

HD = 128
SIDE = 4
TOKENS = 65
ROWS = 72
LANES = 128
ROUTES = 4
PIECES = 5
NEG_FILL = -1e30
MIB = 1 << 20
BF = jnp.bfloat16
F32 = jnp.float32
NT = (((1,), (1,)), ((), ()))


def vmem(limit):
    return pltpu.CompilerParams(vmem_limit_bytes=limit * MIB)


def dot(a, b):
    return jnp.dot(a, b, preferred_element_type=F32)


def dot_nt(a, b):
    return lax.dot_general(a, b, NT, preferred_element_type=F32)


def attention_kernel(mine, *refs):
    given, outs, held_in = refs[:6], refs[6 : 6 + 2 * SIDE], refs[6 + 2 * SIDE : 13 + 2 * SIDE]
    scores, mixed_rows, blocks, made, sems = refs[13 + 2 * SIDE :]
    scale = HD ** (-0.5)
    pool = given[5]
    sources = [*given[:5], pool.at[0], pool.at[1]]
    copies = [
        pltpu.make_async_copy(source, buf, sems.at[i])
        for i, (source, buf) in enumerate(zip(sources, held_in))
    ]
    for c in copies:
        c.start()
    pre, lens, table, dec, weight, keys, values = held_in
    copies[0].wait()
    spans, _, span, _ = pre.shape
    part = span // 2
    for r in range(spans):
        for h in range(2):
            width = part * (h + 1)
            q = pre[r, 0, h * part : (h + 1) * part, :]
            k = pre[r, 1, :width, :]
            v = pre[r, 2, :width, :]
            s = dot_nt(q, k) * scale
            row = lax.broadcasted_iota(jnp.int32, s.shape, 0) + h * part
            col = lax.broadcasted_iota(jnp.int32, s.shape, 1)
            s = jnp.where(col <= row, s, NEG_FILL)
            p = jnp.exp(s - jnp.max(s, axis=-1, keepdims=True))
            w = (p / jnp.sum(p, axis=-1, keepdims=True)).astype(BF)
            at = r * span + h * part
            mixed_rows[at : at + part, :] = dot(w, v).astype(BF).astype(F32)
    for c in copies[1:5]:
        c.wait()
    requests, entries = table.shape
    pages, page = keys.shape[0], keys.shape[1]
    square = (requests, requests)
    diagonal = lax.broadcasted_iota(jnp.int32, square, 0) == lax.broadcasted_iota(jnp.int32, square, 1)
    lengths = jnp.where(diagonal, jnp.broadcast_to(lens[...], square), 0).astype(F32)
    lengths = jnp.sum(lengths, axis=1, keepdims=True).astype(jnp.int32)
    held = jnp.clip(
        lengths - page * lax.broadcasted_iota(jnp.int32, (requests, entries), 1), 0, page
    )
    ids = table[...]
    lane = lax.broadcasted_iota(jnp.int32, (requests, page), 1)
    limit = jnp.zeros((requests, page), jnp.int32)
    for j in range(entries):
        limit = limit + jnp.where(ids[:, j : j + 1] == lane, held[:, j : j + 1], 0)
    q = dec[0]
    own = jnp.sum(q.astype(F32) * dec[1].astype(F32), axis=-1, keepdims=True) * scale
    group = 4
    wide = group * page
    copies[5].wait()
    top = jnp.full((requests, wide), NEG_FILL, F32)
    for c in range(pages // group):
        k = keys[c * group : (c + 1) * group].reshape(wide, HD)
        s = dot_nt(q, k) * scale
        s = jnp.concatenate(
            [
                jnp.where(
                    lane < limit[:, c * group + g : c * group + g + 1],
                    s[:, g * page : (g + 1) * page],
                    NEG_FILL,
                )
                for g in range(group)
            ],
            axis=1,
        )
        scores[:, c * wide : (c + 1) * wide] = s
        top = jnp.maximum(top, s)
    top = jnp.maximum(jnp.max(top, axis=-1, keepdims=True), own)
    total = jnp.zeros((requests, wide), F32)
    for c in range(pages // group):
        p = jnp.exp(scores[:, c * wide : (c + 1) * wide] - top)
        scores[:, c * wide : (c + 1) * wide] = p
        total = total + p
    own = jnp.exp(own - top)
    total = jnp.sum(total, axis=-1, keepdims=True) + own
    copies[6].wait()
    mixed = (own / total).astype(BF).astype(F32) * dec[2].astype(F32)
    for c in range(pages // group):
        w = (scores[:, c * wide : (c + 1) * wide] / total).astype(BF)
        mixed = mixed + dot(w, values[c * group : (c + 1) * group].reshape(wide, HD))
    mixed_rows[spans * span : spans * span + requests, :] = mixed.astype(BF).astype(F32)

    real = lax.broadcasted_iota(jnp.int32, (ROWS, HD), 0) < TOKENS
    for i in range(SIDE * SIDE):
        blocks[i] = jnp.where(real, mixed_rows[i * TOKENS : i * TOKENS + ROWS, :], 0.0)
    half = weight.shape[1] // 2
    at_x, at_z = mine[0] // SIDE, mine[0] % SIDE

    def rows(picked):
        return jnp.concatenate([blocks[i] for i in picked], axis=0).astype(BF)

    xs = [jnp.bitwise_xor(at_x, d) * SIDE for d in range(SIDE)]
    zs = [jnp.bitwise_xor(at_z, d) for d in range(SIDE)]
    leaving = [
        pltpu.make_async_copy(made.at[i], out, sems.at[len(copies) + i]) for i, out in enumerate(outs)
    ]
    for d in (2, 1, 3, 0):
        made[d] = dot(rows([xs[d] + z for z in zs]), weight[:, :half]).astype(BF)
        leaving[d].start()
        made[SIDE + d] = dot(rows([x + zs[d] for x in xs]), weight[:, half:]).astype(BF)
        leaving[SIDE + d].start()
    for c in leaving:
        c.wait()


def attention(mine, prefill_qkv, decode_qkv, cache_pool, page_table, cache_len, out_weight):
    requests = decode_qkv.shape[0]
    pages, page = cache_pool.shape[1:3]
    half = out_weight.shape[1] // 2
    given = [
        prefill_qkv,
        cache_len[None, :],
        page_table,
        decode_qkv.transpose(1, 0, 2),
        out_weight,
        cache_pool,
    ]
    return pl.pallas_call(
        attention_kernel,
        out_shape=[jax.ShapeDtypeStruct((SIDE * ROWS, half), BF)] * (2 * SIDE),
        in_specs=[pl.BlockSpec(memory_space=pltpu.SMEM)]
        + [pl.BlockSpec(memory_space=pltpu.HBM)] * len(given),
        out_specs=[pl.BlockSpec(memory_space=pltpu.HBM)] * (2 * SIDE),
        scratch_shapes=[pltpu.VMEM(a.shape, a.dtype) for a in given[:5]]
        + [
            pltpu.VMEM((pages, page, HD), BF),
            pltpu.VMEM((pages, page, HD), BF),
            pltpu.VMEM((requests, pages * page), F32),
            pltpu.VMEM((SIDE * SIDE * TOKENS + 8, HD), F32),
            pltpu.VMEM((SIDE * SIDE, ROWS, HD), F32),
            pltpu.VMEM((2 * SIDE, SIDE * ROWS, half), BF),
            pltpu.SemaphoreType.DMA((7 + 2 * SIDE,)),
        ],
        compiler_params=vmem(56),
        name="attention",
    )(mine, *given)


def along_x(a, d):
    return lax.ppermute(a, "exp", [(i, i ^ (d * SIDE)) for i in range(SIDE * SIDE)])


def along_z(a, d):
    return lax.ppermute(a, "exp", [(i, i ^ d) for i in range(SIDE * SIDE)])


def add_up(parts):
    total = parts[0].astype(F32)
    for p in parts[1:]:
        total = total + p.astype(F32)
    return total


def ring_sum(parts, along):
    half = parts[0].shape[0] // 2
    near = along(parts[2][:half], 1)
    far = along(parts[2][half:], 3)
    one = jnp.concatenate([parts[1][:half], add_up([parts[1][half:], far]).astype(BF)], axis=0)
    three = jnp.concatenate([add_up([parts[3][:half], near]).astype(BF), parts[3][half:]], axis=0)
    return one, three


def sum_first(parts):
    parts_a, parts_b = parts[:SIDE], parts[SIDE:]
    one_a, three_a = ring_sum(parts_a, along_x)
    one_b, three_b = ring_sum(parts_b, along_z)
    one_a, three_a, one_b, three_b = lax.optimization_barrier((one_a, three_a, one_b, three_b))
    got_a = [parts_a[0], along_x(one_a, 1), along_x(three_a, 3)]
    got_b = [parts_b[0], along_z(one_b, 1), along_z(three_b, 3)]
    sum_a = add_up(got_a).astype(BF).reshape(SIDE, ROWS, -1)
    sum_b = add_up(got_b).astype(BF).reshape(SIDE, ROWS, -1)
    return sum_a, sum_b


def sum_second(sum_a, sum_b):
    got_a, got_b = [sum_a[0]], [sum_b[0]]
    for d in (1, 3, 2):
        got_a.append(along_z(sum_a[d], d))
        got_b.append(along_x(sum_b[d], d))
    return got_a, got_b


def gather(rows):
    half = rows.shape[1] // 2
    rows_a, rows_b = rows[:, :half], rows[:, half:]
    got_a, got_b = {0: rows_a}, {0: rows_b}
    for d in (1, 3, 2):
        got_a[d] = along_z(rows_a, d)
        got_b[d] = along_x(rows_b, d)
    rows_a = jnp.stack([got_a[d] for d in range(SIDE)])
    rows_b = jnp.stack([got_b[d] for d in range(SIDE)])
    rows_a, rows_b = lax.optimization_barrier((rows_a, rows_b))
    one_a, one_b = along_x(rows_a, 1), along_z(rows_b, 1)
    three_a, three_b = along_x(rows_a, 3), along_z(rows_b, 3)
    half = SIDE // 2
    return (
        [rows_a, one_a, three_a, along_x(three_a[:half], 1), along_x(one_a[half:], 3)],
        [rows_b, one_b, three_b, along_z(three_b[:half], 1), along_z(one_b[half:], 3)],
    )


def block_of(pieces, d, i):
    if d == 2:
        return pieces[3][i] if i < SIDE // 2 else pieces[4][i - SIDE // 2]
    return pieces[{0: 0, 1: 1, 3: 2}[d]][i]


def token_kernel(a0, a1, a2, a3, b0, b1, b2, b3, residual, gain, tags, stream, normed):
    f = lambda r: r[...].astype(F32)
    projected = jnp.concatenate(
        [f(a0) + f(a1) + f(a2) + f(a3), f(b0) + f(b1) + f(b2) + f(b3)], axis=1
    )
    held = (f(residual) + projected).astype(BF)
    stream[...] = held
    wide = held.astype(F32)
    mean = jnp.mean(wide * wide, axis=-1, keepdims=True)
    rows = wide * lax.rsqrt(mean + 1e-06) * gain[...]
    normed[...] = rows.astype(BF)
    count, lanes = tags.shape
    is_tag = lax.broadcasted_iota(jnp.int32, (count, lanes), 0) >= TOKENS
    normed[:, :lanes] = jnp.where(is_tag, tags[...], rows[:, :lanes]).astype(BF)


def chosen_rows(mine, rows_a, columns, capacity):
    shape = (columns, LANES)
    expert = lax.broadcasted_iota(jnp.int32, shape, 0) * (SIDE * SIDE // 2) + mine // 2
    expert = expert.astype(F32)
    hits = []
    for x in range(SIDE):
        for z in range(SIDE):
            tags = block_of(rows_a, x, z)[:, :LANES].astype(F32)
            hit = jnp.zeros(shape, F32)
            for k in range(ROUTES):
                named = jnp.broadcast_to(tags[TOKENS + k : TOKENS + k + 1, :], shape)
                hit = jnp.where(named == expert, 1.0, hit)
            hits.append(hit)
    hits = jnp.concatenate(hits, axis=0)
    before = lax.broadcasted_iota(jnp.int32, (LANES, LANES), 0) < lax.broadcasted_iota(
        jnp.int32, (LANES, LANES), 1
    )
    rank = dot(hits.astype(BF), before.astype(F32).astype(BF))
    rank = jnp.where(hits > 0.0, rank, -1.0)
    slot = lax.broadcasted_iota(jnp.int32, (columns, capacity, LANES), 1).astype(F32)
    chosen = []
    for i in range(SIDE * SIDE):
        here = rank[i * columns : (i + 1) * columns, :]
        here = jnp.broadcast_to(here[:, None, :], (columns, capacity, LANES))
        here = jnp.where(here == slot, 1.0, 0.0).reshape(columns * capacity, LANES)
        chosen.append(here[:, :ROWS].astype(BF))
    return chosen


def pick_kernel(mine, *refs):
    rows_a, rows_b, out = refs[:PIECES], refs[PIECES : 2 * PIECES], refs[-1]
    columns, _, capacity, width = out.shape
    half = width // 2
    chosen = chosen_rows(mine[0], rows_a, columns, capacity)
    for x in range(SIDE):
        for z in range(SIDE):
            block = jnp.bitwise_xor(mine[0], x * SIDE + z)
            pick = chosen[x * SIDE + z]
            a = dot(pick, block_of(rows_a, x, z)).reshape(columns, capacity, half).astype(BF)
            b = dot(pick, block_of(rows_b, z, x)).reshape(columns, capacity, half).astype(BF)
            for r in range(columns):
                out[r, block, :, :half] = a[r]
                out[r, block, :, half:] = b[r]


def pick(mine, rows_a, rows_b, columns, capacity):
    width = 2 * rows_a[0].shape[-1]
    whole = pl.BlockSpec(memory_space=pltpu.VMEM)
    return pl.pallas_call(
        pick_kernel,
        out_shape=jax.ShapeDtypeStruct((columns, SIDE * SIDE, capacity, width), BF),
        in_specs=[pl.BlockSpec(memory_space=pltpu.SMEM)] + [whole] * (2 * PIECES),
        out_specs=whole,
        compiler_params=vmem(56),
        name="pick",
    )(mine, *rows_a, *rows_b)


def expert_kernel(rows, gate_up, down, out, gate_held, up_held, down_held, sems):
    sources = (gate_up.at[0, 0], gate_up.at[0, 1], down.at[0])
    copies = [
        pltpu.make_async_copy(source, buf, sems.at[i])
        for i, (source, buf) in enumerate(zip(sources, (gate_held, up_held, down_held)))
    ]
    first = pl.program_id(0) == 0

    @pl.when(first)
    def _():
        for c in copies:
            c.start()
        copies[0].wait()

    x = rows[...]
    gate = dot_nt(x, gate_held[...])

    @pl.when(first)
    def _():
        copies[1].wait()

    up = dot_nt(x, up_held[...])
    hidden = (gate / (1.0 + jnp.exp(-gate)) * up).astype(BF)

    @pl.when(first)
    def _():
        copies[2].wait()

    out[...] = dot(hidden, down_held[...]).astype(BF)


def experts(rows, gate_up, down):
    count, width = rows.shape
    step = 512
    return pl.pallas_call(
        expert_kernel,
        grid=(count // step,),
        out_shape=jax.ShapeDtypeStruct((count, width), BF),
        in_specs=[
            pl.BlockSpec((step, width), lambda i: (i, 0)),
            pl.BlockSpec(memory_space=pltpu.HBM),
            pl.BlockSpec(memory_space=pltpu.HBM),
        ],
        out_specs=pl.BlockSpec((step, width), lambda i: (i, 0)),
        scratch_shapes=[
            pltpu.VMEM(gate_up.shape[2:], BF),
            pltpu.VMEM(gate_up.shape[2:], BF),
            pltpu.VMEM(down.shape[1:], BF),
            pltpu.SemaphoreType.DMA((3,)),
        ],
        compiler_params=vmem(56),
        cost_estimate=pl.CostEstimate(
            flops=6 * count * width * down.shape[1],
            bytes_accessed=2 * (2 * count * width + 3 * width * down.shape[1]),
            transcendentals=count * down.shape[1],
        ),
        name="experts",
    )(rows, gate_up, down)


def result_kernel(mix, rows, base, out):
    routed = dot(mix[...], rows[...])
    total = routed[:ROWS] + routed[ROWS:] + base[...]
    out[...] = total[: out.shape[0]].astype(BF)


def result(mix, rows, base, tok_rows):
    count, width = rows.shape
    step = 512
    return pl.pallas_call(
        result_kernel,
        grid=(width // step,),
        out_shape=jax.ShapeDtypeStruct((tok_rows, width), BF),
        in_specs=[
            pl.BlockSpec(mix.shape, lambda i: (0, 0)),
            pl.BlockSpec((count, step), lambda i: (0, i)),
            pl.BlockSpec((ROWS, step), lambda i: (0, i)),
        ],
        out_specs=pl.BlockSpec((tok_rows, step), lambda i: (0, i)),
        compiler_params=vmem(32),
        name="result",
    )(mix, rows, base)


def shared_kernel(*refs):
    rows_a, rows_b = refs[:PIECES], refs[PIECES : 2 * PIECES]
    gate_up, down = refs[2 * PIECES : 2 * PIECES + 2]
    outs, hidden = refs[2 * PIECES + 2 : -1], refs[-1]
    half = down.shape[1] // 2
    for x in range(SIDE):
        a, b = (
            jnp.concatenate(blocks, axis=0).astype(BF)
            for blocks in (
                [block_of(rows_a, x, z).astype(F32) for z in range(SIDE)],
                [block_of(rows_b, z, x).astype(F32) for z in range(SIDE)],
            )
        )
        gate = dot_nt(a, gate_up[0, :, :half]) + dot_nt(b, gate_up[0, :, half:])
        up = dot_nt(a, gate_up[1, :, :half]) + dot_nt(b, gate_up[1, :, half:])
        hidden[x] = (gate / (1.0 + jnp.exp(-gate)) * up).reshape(SIDE, ROWS, -1)
    for d in range(SIDE):
        part = hidden[d].reshape(SIDE * ROWS, -1)
        outs[d][...] = dot(part.astype(BF), down[:, :half]).astype(BF)
        part = hidden[:, d].reshape(SIDE * ROWS, -1)
        outs[SIDE + d][...] = dot(part.astype(BF), down[:, half:]).astype(BF)


def shared_expert(rows_a, rows_b, gate_up, down):
    half = down.shape[1] // 2
    count, width = SIDE * SIDE * ROWS, down.shape[1]
    return pl.pallas_call(
        shared_kernel,
        out_shape=[jax.ShapeDtypeStruct((SIDE * ROWS, half), BF)] * (2 * SIDE),
        scratch_shapes=[pltpu.VMEM((SIDE, SIDE, ROWS, down.shape[0]), F32)],
        compiler_params=vmem(48),
        cost_estimate=pl.CostEstimate(
            flops=6 * count * width * down.shape[0],
            bytes_accessed=2 * (2 * count * width + 3 * width * down.shape[0]),
            transcendentals=count * down.shape[0],
        ),
        name="shared_expert",
    )(*rows_a, *rows_b, gate_up, down)


def on_device(
    residual,
    prefill_qkv,
    decode_qkv,
    cache_pool,
    page_table,
    cache_len,
    out_weight,
    norm_gain,
    shared_gate_up,
    shared_down,
    shared_gate,
    routes,
    route_weight,
    expert_gate_up,
    expert_down,
):
    mine = lax.axis_index("exp")
    groups = lax.axis_size("exp")
    tok_rows, width = residual.shape
    devices = groups * lax.axis_size("req")
    experts_all = devices // 2
    route_count = routes.shape[1]
    capacity = 8

    flat = routes.reshape(-1)
    place = jnp.arange(flat.shape[0], dtype=jnp.int32)
    same = (flat[:, None] == flat[None, :]) & (place[None, :] < place[:, None])
    rank = jnp.sum(same.astype(jnp.int32), axis=1)
    slot_of = (flat * capacity + rank).reshape(tok_rows, route_count)
    slot_of = jnp.pad(slot_of, ((0, ROWS - tok_rows), (0, 0)), constant_values=-1)
    weight = jnp.pad(route_weight, ((0, ROWS - tok_rows), (0, 0)))
    tags = jnp.pad(
        routes.T.astype(F32),
        ((tok_rows, ROWS - tok_rows - route_count), (0, LANES - tok_rows)),
        constant_values=-1.0,
    )
    columns = jnp.arange(devices * capacity, dtype=jnp.int32)
    columns = columns // (2 * capacity) * capacity + columns % capacity
    mix = jnp.sum(
        jnp.where(slot_of[:, :, None] == columns[None, None, :], weight[:, :, None], 0.0), axis=1
    )
    mix_high = mix.astype(BF)
    mix_low = (mix - mix_high.astype(F32)).astype(BF)
    mix = jnp.concatenate([mix_high, mix_low], axis=0)

    parts = attention(
        mine[None], prefill_qkv, decode_qkv, cache_pool, page_table, cache_len, out_weight
    )
    sums = sum_first(parts)
    got_a, got_b = sum_second(*lax.optimization_barrier(sums))
    stream, normed = pl.pallas_call(
        token_kernel,
        out_shape=[jax.ShapeDtypeStruct((ROWS, width), BF)] * 2,
        compiler_params=vmem(32),
        name="token_rows",
    )(
        *got_a,
        *got_b,
        jnp.pad(residual, ((0, ROWS - tok_rows), (0, 0))),
        norm_gain[None, :],
        tags,
    )
    rows_a, rows_b = gather(normed)
    outgoing = pick(mine[None], rows_a, rows_b, lax.axis_size("req"), capacity)
    arrived = lax.all_to_all(
        outgoing.reshape(lax.axis_size("req"), groups * capacity, width),
        "req",
        split_axis=0,
        concat_axis=0,
        tiled=True,
    )
    sums = sum_first(shared_expert(rows_a, rows_b, shared_gate_up.transpose(0, 2, 1), shared_down))
    got_a, got_b = sum_second(*lax.optimization_barrier(sums))
    arrived, got_a, got_b = lax.optimization_barrier((arrived, got_a, got_b))
    answer = experts(arrived.reshape(devices * capacity, width), expert_gate_up.transpose(0, 1, 3, 2), expert_down)
    returned = lax.all_to_all(
        answer.reshape(devices, capacity, width),
        ("req", "exp"),
        split_axis=0,
        concat_axis=0,
        tiled=True,
    )
    shared = jnp.concatenate([add_up(got_a), add_up(got_b)], axis=1)
    shared_scale = jax.nn.sigmoid(dot(normed, shared_gate))
    base = stream.astype(F32) + shared_scale[:, None] * shared
    return result(mix, returned.reshape(devices * capacity, width), base, tok_rows)


def solution(mesh):
    placed = (
        P(("req", "exp"), None),
        P("req", None, None, "exp"),
        P("req", None, "exp"),
        P(None, "req", None, "exp"),
        P("req", None),
        P("req"),
        P("exp", None),
        P(),
        P(None, None, "exp"),
        P("exp", None),
        P(),
        P(("req", "exp"), None),
        P(("req", "exp"), None),
        P(("req", "exp"), None, None, None),
        P(("req", "exp"), None, None),
    )
    return jax.shard_map(
        on_device, mesh=mesh, in_specs=placed, out_specs=P(("req", "exp"), None), check_vma=False
    )
```

```python
import functools

import jax
import jax.numpy as jnp
from jax import lax
from jax.experimental import pallas as pl
from jax.experimental.pallas import tpu as pltpu
from jax.sharding import PartitionSpec as P

HD = 128
SIDE = 4
TOKENS = 65
ROWS = 72
LANES = 128
ROUTES = 4
PIECES = 5
NEG_FILL = -1e30
MIB = 1 << 20
BF = jnp.bfloat16
F32 = jnp.float32
NT = (((1,), (1,)), ((), ()))


def vmem(limit):
    return pltpu.CompilerParams(vmem_limit_bytes=limit * MIB)


def dot(a, b):
    return jnp.dot(a, b, preferred_element_type=F32)


def dot_nt(a, b):
    return lax.dot_general(a, b, NT, preferred_element_type=F32)


def attention_kernel(mine, *refs):
    given, outs, held_in = refs[:6], refs[6 : 6 + 2 * PIECES], refs[6 + 2 * PIECES : 13 + 2 * PIECES]
    scores, mixed_rows, blocks, made, sems = refs[13 + 2 * PIECES :]
    scale = HD ** (-0.5)
    pool = given[5]
    sources = [*given[:5], pool.at[0], pool.at[1]]
    copies = [
        pltpu.make_async_copy(source, buf, sems.at[i])
        for i, (source, buf) in enumerate(zip(sources, held_in))
    ]
    for c in copies:
        c.start()
    pre, lens, table, dec, weight, keys, values = held_in
    copies[0].wait()
    spans, _, span, _ = pre.shape
    part = span // 2
    for r in range(spans):
        for h in range(2):
            width = part * (h + 1)
            q = pre[r, 0, h * part : (h + 1) * part, :]
            k = pre[r, 1, :width, :]
            v = pre[r, 2, :width, :]
            s = dot_nt(q, k) * scale
            row = lax.broadcasted_iota(jnp.int32, s.shape, 0) + h * part
            col = lax.broadcasted_iota(jnp.int32, s.shape, 1)
            s = jnp.where(col <= row, s, NEG_FILL)
            p = jnp.exp(s - jnp.max(s, axis=-1, keepdims=True))
            w = (p / jnp.sum(p, axis=-1, keepdims=True)).astype(BF)
            at = r * span + h * part
            mixed_rows[at : at + part, :] = dot(w, v).astype(BF).astype(F32)
    for c in copies[1:5]:
        c.wait()
    requests, entries = table.shape
    pages, page = keys.shape[0], keys.shape[1]
    square = (requests, requests)
    diagonal = lax.broadcasted_iota(jnp.int32, square, 0) == lax.broadcasted_iota(jnp.int32, square, 1)
    lengths = jnp.where(diagonal, jnp.broadcast_to(lens[...], square), 0).astype(F32)
    lengths = jnp.sum(lengths, axis=1, keepdims=True).astype(jnp.int32)
    held = jnp.clip(
        lengths - page * lax.broadcasted_iota(jnp.int32, (requests, entries), 1), 0, page
    )
    ids = table[...]
    lane = lax.broadcasted_iota(jnp.int32, (requests, page), 1)
    limit = jnp.zeros((requests, page), jnp.int32)
    for j in range(entries):
        limit = limit + jnp.where(ids[:, j : j + 1] == lane, held[:, j : j + 1], 0)
    q = dec[0]
    own = jnp.sum(q.astype(F32) * dec[1].astype(F32), axis=-1, keepdims=True) * scale
    group = 4
    wide = group * page
    copies[5].wait()
    top = jnp.full((requests, wide), NEG_FILL, F32)
    for c in range(pages // group):
        k = keys[c * group : (c + 1) * group].reshape(wide, HD)
        s = dot_nt(q, k) * scale
        s = jnp.concatenate(
            [
                jnp.where(
                    lane < limit[:, c * group + g : c * group + g + 1],
                    s[:, g * page : (g + 1) * page],
                    NEG_FILL,
                )
                for g in range(group)
            ],
            axis=1,
        )
        scores[:, c * wide : (c + 1) * wide] = s
        top = jnp.maximum(top, s)
    top = jnp.maximum(jnp.max(top, axis=-1, keepdims=True), own)
    total = jnp.zeros((requests, wide), F32)
    for c in range(pages // group):
        p = jnp.exp(scores[:, c * wide : (c + 1) * wide] - top)
        scores[:, c * wide : (c + 1) * wide] = p
        total = total + p
    own = jnp.exp(own - top)
    total = jnp.sum(total, axis=-1, keepdims=True) + own
    copies[6].wait()
    mixed = (own / total).astype(BF).astype(F32) * dec[2].astype(F32)
    for c in range(pages // group):
        w = (scores[:, c * wide : (c + 1) * wide] / total).astype(BF)
        mixed = mixed + dot(w, values[c * group : (c + 1) * group].reshape(wide, HD))
    mixed_rows[spans * span : spans * span + requests, :] = mixed.astype(BF).astype(F32)

    real = lax.broadcasted_iota(jnp.int32, (ROWS, HD), 0) < TOKENS
    for i in range(SIDE * SIDE):
        blocks[i] = jnp.where(real, mixed_rows[i * TOKENS : i * TOKENS + ROWS, :], 0.0)
    half = weight.shape[1] // 2
    at_x, at_z = mine[0] // SIDE, mine[0] % SIDE

    def rows(picked):
        return jnp.concatenate([blocks[i] for i in picked], axis=0).astype(BF)

    xs = [jnp.bitwise_xor(at_x, d) * SIDE for d in range(SIDE)]
    zs = [jnp.bitwise_xor(at_z, d) for d in range(SIDE)]
    middle = SIDE * ROWS // 2
    sent = []

    def send(at, place, out):
        sent.append(pltpu.make_async_copy(place, out, sems.at[at]))
        sent[-1].start()

    for d in (2, 1, 3, 0):
        for f, picked in enumerate(([xs[d] + z for z in zs], [x + zs[d] for x in xs])):
            i, first = f * SIDE + d, f * PIECES
            made[i] = dot(rows(picked), weight[:, f * half : (f + 1) * half]).astype(BF)
            at = len(copies) + first
            if d == 2:
                send(at + 3, made.at[i, pl.ds(0, middle)], outs[first + 3])
                send(at + 4, made.at[i, pl.ds(middle, middle)], outs[first + 4])
            else:
                place = {0: 0, 1: 1, 3: 2}[d]
                send(at + place, made.at[i], outs[first + place])
    for c in sent:
        c.wait()


def attention(mine, prefill_qkv, decode_qkv, cache_pool, page_table, cache_len, out_weight):
    requests = decode_qkv.shape[0]
    pages, page = cache_pool.shape[1:3]
    half = out_weight.shape[1] // 2
    given = [
        prefill_qkv,
        cache_len[None, :],
        page_table,
        decode_qkv.transpose(1, 0, 2),
        out_weight,
        cache_pool,
    ]
    return pl.pallas_call(
        attention_kernel,
        out_shape=part_shapes(half) * 2,
        in_specs=[pl.BlockSpec(memory_space=pltpu.SMEM)]
        + [pl.BlockSpec(memory_space=pltpu.HBM)] * len(given),
        out_specs=[pl.BlockSpec(memory_space=pltpu.HBM)] * (2 * PIECES),
        scratch_shapes=[pltpu.VMEM(a.shape, a.dtype) for a in given[:5]]
        + [
            pltpu.VMEM((pages, page, HD), BF),
            pltpu.VMEM((pages, page, HD), BF),
            pltpu.VMEM((requests, pages * page), F32),
            pltpu.VMEM((SIDE * SIDE * TOKENS + 8, HD), F32),
            pltpu.VMEM((SIDE * SIDE, ROWS, HD), F32),
            pltpu.VMEM((2 * SIDE, SIDE * ROWS, half), BF),
            pltpu.SemaphoreType.DMA((7 + 2 * PIECES,)),
        ],
        compiler_params=vmem(56),
        name="attention",
    )(mine, *given)


def along_x(a, d):
    return lax.ppermute(a, "exp", [(i, i ^ (d * SIDE)) for i in range(SIDE * SIDE)])


def along_z(a, d):
    return lax.ppermute(a, "exp", [(i, i ^ d) for i in range(SIDE * SIDE)])


def add_up(parts):
    total = parts[0].astype(F32)
    for p in parts[1:]:
        total = total + p.astype(F32)
    return total


def part_shapes(half):
    rows = SIDE * ROWS
    return [jax.ShapeDtypeStruct((n, half), BF) for n in (rows, rows, rows, rows // 2, rows // 2)]


def ring_sum(parts, along):
    half = parts[3].shape[0]
    near = along(parts[3], 1)
    far = along(parts[4], 3)
    one = jnp.concatenate([parts[1][:half], add_up([parts[1][half:], far]).astype(BF)], axis=0)
    three = jnp.concatenate([add_up([parts[2][:half], near]).astype(BF), parts[2][half:]], axis=0)
    return one, three


def sum_first(parts):
    parts_a, parts_b = parts[:PIECES], parts[PIECES:]
    one_a, three_a = ring_sum(parts_a, along_x)
    one_b, three_b = ring_sum(parts_b, along_z)
    one_a, three_a, one_b, three_b = lax.optimization_barrier((one_a, three_a, one_b, three_b))
    got_a = [parts_a[0], along_x(one_a, 1), along_x(three_a, 3)]
    got_b = [parts_b[0], along_z(one_b, 1), along_z(three_b, 3)]
    sum_a = add_up(got_a).astype(BF).reshape(SIDE, ROWS, -1)
    sum_b = add_up(got_b).astype(BF).reshape(SIDE, ROWS, -1)
    return sum_a, sum_b


def sum_second(sum_a, sum_b):
    got_a, got_b = [sum_a[0]], [sum_b[0]]
    for d in (1, 3, 2):
        got_a.append(along_z(sum_a[d], d))
        got_b.append(along_x(sum_b[d], d))
    return got_a, got_b


def gather(rows):
    half = rows.shape[1] // 2
    rows_a, rows_b = rows[:, :half], rows[:, half:]
    got_a, got_b = {0: rows_a}, {0: rows_b}
    for d in (1, 3, 2):
        got_a[d] = along_z(rows_a, d)
        got_b[d] = along_x(rows_b, d)
    rows_a = jnp.stack([got_a[d] for d in range(SIDE)])
    rows_b = jnp.stack([got_b[d] for d in range(SIDE)])
    rows_a, rows_b = lax.optimization_barrier((rows_a, rows_b))
    one_a, one_b = along_x(rows_a, 1), along_z(rows_b, 1)
    three_a, three_b = along_x(rows_a, 3), along_z(rows_b, 3)
    half = SIDE // 2
    return (
        [rows_a, one_a, three_a, along_x(three_a[:half], 1), along_x(one_a[half:], 3)],
        [rows_b, one_b, three_b, along_z(three_b[:half], 1), along_z(one_b[half:], 3)],
    )


def block_of(pieces, d, i):
    if d == 2:
        return pieces[3][i] if i < SIDE // 2 else pieces[4][i - SIDE // 2]
    return pieces[{0: 0, 1: 1, 3: 2}[d]][i]


def token_kernel(a0, a1, a2, a3, b0, b1, b2, b3, residual, gain, tags, stream, normed):
    f = lambda r: r[...].astype(F32)
    projected = jnp.concatenate(
        [f(a0) + f(a1) + f(a2) + f(a3), f(b0) + f(b1) + f(b2) + f(b3)], axis=1
    )
    held = (f(residual) + projected).astype(BF)
    stream[...] = held
    wide = held.astype(F32)
    mean = jnp.mean(wide * wide, axis=-1, keepdims=True)
    rows = wide * lax.rsqrt(mean + 1e-06) * gain[...]
    normed[...] = rows.astype(BF)
    count, lanes = tags.shape
    is_tag = lax.broadcasted_iota(jnp.int32, (count, lanes), 0) >= TOKENS
    normed[:, :lanes] = jnp.where(is_tag, tags[...], rows[:, :lanes]).astype(BF)


def chosen_rows(mine, rows_a, columns, capacity):
    shape = (columns, LANES)
    expert = lax.broadcasted_iota(jnp.int32, shape, 0) * (SIDE * SIDE // 2) + mine // 2
    expert = expert.astype(F32)
    hits = []
    for x in range(SIDE):
        for z in range(SIDE):
            tags = block_of(rows_a, x, z)[:, :LANES].astype(F32)
            hit = jnp.zeros(shape, F32)
            for k in range(ROUTES):
                named = jnp.broadcast_to(tags[TOKENS + k : TOKENS + k + 1, :], shape)
                hit = jnp.where(named == expert, 1.0, hit)
            hits.append(hit)
    hits = jnp.concatenate(hits, axis=0)
    before = lax.broadcasted_iota(jnp.int32, (LANES, LANES), 0) < lax.broadcasted_iota(
        jnp.int32, (LANES, LANES), 1
    )
    rank = dot(hits.astype(BF), before.astype(F32).astype(BF))
    rank = jnp.where(hits > 0.0, rank, -1.0)
    slot = lax.broadcasted_iota(jnp.int32, (columns, capacity, LANES), 1).astype(F32)
    chosen = []
    for i in range(SIDE * SIDE):
        here = rank[i * columns : (i + 1) * columns, :]
        here = jnp.broadcast_to(here[:, None, :], (columns, capacity, LANES))
        here = jnp.where(here == slot, 1.0, 0.0).reshape(columns * capacity, LANES)
        chosen.append(here[:, :ROWS].astype(BF))
    return chosen


def pick_kernel(mine, *refs):
    rows_a, rows_b, out = refs[:PIECES], refs[PIECES : 2 * PIECES], refs[-1]
    columns, _, capacity, width = out.shape
    half = width // 2
    chosen = chosen_rows(mine[0], rows_a, columns, capacity)
    for x in range(SIDE):
        for z in range(SIDE):
            block = jnp.bitwise_xor(mine[0], x * SIDE + z)
            pick = chosen[x * SIDE + z]
            a = dot(pick, block_of(rows_a, x, z)).reshape(columns, capacity, half).astype(BF)
            b = dot(pick, block_of(rows_b, z, x)).reshape(columns, capacity, half).astype(BF)
            for r in range(columns):
                out[r, block, :, :half] = a[r]
                out[r, block, :, half:] = b[r]


def pick(mine, rows_a, rows_b, columns, capacity):
    width = 2 * rows_a[0].shape[-1]
    whole = pl.BlockSpec(memory_space=pltpu.VMEM)
    return pl.pallas_call(
        pick_kernel,
        out_shape=jax.ShapeDtypeStruct((columns, SIDE * SIDE, capacity, width), BF),
        in_specs=[pl.BlockSpec(memory_space=pltpu.SMEM)] + [whole] * (2 * PIECES),
        out_specs=whole,
        compiler_params=vmem(56),
        name="pick",
    )(mine, *rows_a, *rows_b)


def expert_kernel(rows, gate_up, down, out):
    x = rows[...]
    gate = dot_nt(x, gate_up[0, 0])
    up = dot_nt(x, gate_up[0, 1])
    hidden = (gate / (1.0 + jnp.exp(-gate)) * up).astype(BF)
    out[...] = dot(hidden, down[0]).astype(BF)


def experts(rows, gate_up, down):
    count, width = rows.shape
    step = 512
    return pl.pallas_call(
        expert_kernel,
        grid=(count // step,),
        out_shape=jax.ShapeDtypeStruct((count, width), BF),
        in_specs=[
            pl.BlockSpec((step, width), lambda i: (i, 0)),
            pl.BlockSpec(gate_up.shape, lambda i: (0, 0, 0, 0)),
            pl.BlockSpec(down.shape, lambda i: (0, 0, 0)),
        ],
        out_specs=pl.BlockSpec((step, width), lambda i: (i, 0)),
        compiler_params=vmem(56),
        cost_estimate=pl.CostEstimate(
            flops=6 * count * width * down.shape[1],
            bytes_accessed=2 * (2 * count * width + 3 * width * down.shape[1]),
            transcendentals=count * down.shape[1],
        ),
        name="experts",
    )(rows, gate_up, down)


def shared_kernel(*refs):
    rows_a, rows_b = refs[:PIECES], refs[PIECES : 2 * PIECES]
    gate_up, down = refs[2 * PIECES : 2 * PIECES + 2]
    outs, hidden = refs[2 * PIECES + 2 : -1], refs[-1]
    half = down.shape[1] // 2
    for x in range(SIDE):
        a, b = (
            jnp.concatenate(blocks, axis=0).astype(BF)
            for blocks in (
                [block_of(rows_a, x, z).astype(F32) for z in range(SIDE)],
                [block_of(rows_b, z, x).astype(F32) for z in range(SIDE)],
            )
        )
        gate = dot_nt(a, gate_up[0, :, :half]) + dot_nt(b, gate_up[0, :, half:])
        up = dot_nt(a, gate_up[1, :, :half]) + dot_nt(b, gate_up[1, :, half:])
        hidden[x] = (gate / (1.0 + jnp.exp(-gate)) * up).reshape(SIDE, ROWS, -1)
    middle = SIDE * ROWS // 2
    for d in range(SIDE):
        for f, part in enumerate((hidden[d], hidden[:, d])):
            part = part.reshape(SIDE * ROWS, -1).astype(BF)
            made = dot(part, down[:, f * half : (f + 1) * half]).astype(BF)
            if d == 2:
                outs[f * PIECES + 3][...] = made[:middle]
                outs[f * PIECES + 4][...] = made[middle:]
            else:
                outs[f * PIECES + {0: 0, 1: 1, 3: 2}[d]][...] = made


def shared_expert(rows_a, rows_b, gate_up, down):
    half = down.shape[1] // 2
    count, width = SIDE * SIDE * ROWS, down.shape[1]
    return pl.pallas_call(
        shared_kernel,
        out_shape=part_shapes(half) * 2,
        scratch_shapes=[pltpu.VMEM((SIDE, SIDE, ROWS, down.shape[0]), F32)],
        compiler_params=vmem(48),
        cost_estimate=pl.CostEstimate(
            flops=6 * count * width * down.shape[0],
            bytes_accessed=2 * (2 * count * width + 3 * width * down.shape[0]),
            transcendentals=count * down.shape[0],
        ),
        name="shared_expert",
    )(*rows_a, *rows_b, gate_up, down)


def on_device(
    residual,
    prefill_qkv,
    decode_qkv,
    cache_pool,
    page_table,
    cache_len,
    out_weight,
    norm_gain,
    shared_gate_up,
    shared_down,
    shared_gate,
    routes,
    route_weight,
    expert_gate_up,
    expert_down,
):
    mine = lax.axis_index("exp")
    groups = lax.axis_size("exp")
    tok_rows, width = residual.shape
    devices = groups * lax.axis_size("req")
    experts_all = devices // 2
    route_count = routes.shape[1]
    capacity = 8

    flat = routes.reshape(-1)
    place = jnp.arange(flat.shape[0], dtype=jnp.int32)
    same = (flat[:, None] == flat[None, :]) & (place[None, :] < place[:, None])
    rank = jnp.sum(same.astype(jnp.int32), axis=1)
    slot_of = (flat * capacity + rank).reshape(tok_rows, route_count)
    slot_of = jnp.pad(slot_of, ((0, ROWS - tok_rows), (0, 0)), constant_values=-1)
    weight = jnp.pad(route_weight, ((0, ROWS - tok_rows), (0, 0)))
    tags = jnp.pad(
        routes.T.astype(F32),
        ((tok_rows, ROWS - tok_rows - route_count), (0, LANES - tok_rows)),
        constant_values=-1.0,
    )
    columns = jnp.arange(devices * capacity, dtype=jnp.int32)
    columns = columns // (2 * capacity) * capacity + columns % capacity
    mix = jnp.sum(
        jnp.where(slot_of[:, :, None] == columns[None, None, :], weight[:, :, None], 0.0), axis=1
    )
    mix_high = mix.astype(BF)
    mix_low = (mix - mix_high.astype(F32)).astype(BF)
    mix = jnp.concatenate([mix_high, mix_low], axis=0)

    parts = attention(
        mine[None], prefill_qkv, decode_qkv, cache_pool, page_table, cache_len, out_weight
    )
    sums = sum_first(parts)
    got_a, got_b = sum_second(*lax.optimization_barrier(sums))
    stream, normed = pl.pallas_call(
        token_kernel,
        out_shape=[jax.ShapeDtypeStruct((ROWS, width), BF)] * 2,
        compiler_params=vmem(32),
        name="token_rows",
    )(
        *got_a,
        *got_b,
        jnp.pad(residual, ((0, ROWS - tok_rows), (0, 0))),
        norm_gain[None, :],
        tags,
    )
    rows_a, rows_b = gather(normed)
    outgoing = pick(mine[None], rows_a, rows_b, lax.axis_size("req"), capacity)
    arrived = lax.all_to_all(
        outgoing.reshape(lax.axis_size("req"), groups * capacity, width),
        "req",
        split_axis=0,
        concat_axis=0,
        tiled=True,
    )
    sums = sum_first(shared_expert(rows_a, rows_b, shared_gate_up.transpose(0, 2, 1), shared_down))
    got_a, got_b = sum_second(*lax.optimization_barrier(sums))
    arrived, got_a, got_b = lax.optimization_barrier((arrived, got_a, got_b))
    answer = experts(arrived.reshape(devices * capacity, width), expert_gate_up.transpose(0, 1, 3, 2), expert_down)
    returned = lax.all_to_all(
        answer.reshape(devices, capacity, width),
        ("req", "exp"),
        split_axis=0,
        concat_axis=0,
        tiled=True,
    )
    shared = jnp.concatenate([add_up(got_a), add_up(got_b)], axis=1)
    shared_scale = jax.nn.sigmoid(dot(normed, shared_gate))
    routed = dot(mix, returned.reshape(devices * capacity, width))
    routed = routed[:ROWS] + routed[ROWS:]
    result = stream.astype(F32) + routed + shared_scale[:, None] * shared
    return result[:tok_rows].astype(BF)


def solution(mesh):
    placed = (
        P(("req", "exp"), None),
        P("req", None, None, "exp"),
        P("req", None, "exp"),
        P(None, "req", None, "exp"),
        P("req", None),
        P("req"),
        P("exp", None),
        P(),
        P(None, None, "exp"),
        P("exp", None),
        P(),
        P(("req", "exp"), None),
        P(("req", "exp"), None),
        P(("req", "exp"), None, None, None),
        P(("req", "exp"), None, None),
    )
    return jax.shard_map(
        on_device, mesh=mesh, in_specs=placed, out_specs=P(("req", "exp"), None), check_vma=False
    )
```

```python
import functools

import jax
import jax.numpy as jnp
from jax import lax
from jax.experimental import pallas as pl
from jax.experimental.pallas import tpu as pltpu
from jax.sharding import PartitionSpec as P

HD = 128
SIDE = 4
TOKENS = 65
ROWS = 72
LANES = 128
ROUTES = 4
PIECES = 5
NEG_FILL = -1e30
MIB = 1 << 20
BF = jnp.bfloat16
F32 = jnp.float32
NT = (((1,), (1,)), ((), ()))


def vmem(limit):
    return pltpu.CompilerParams(vmem_limit_bytes=limit * MIB)


def dot(a, b):
    return jnp.dot(a, b, preferred_element_type=F32)


def dot_nt(a, b):
    return lax.dot_general(a, b, NT, preferred_element_type=F32)


def attention_kernel(mine, *refs):
    given, outs, held_in = refs[:6], refs[6 : 6 + 2 * PIECES], refs[6 + 2 * PIECES : 13 + 2 * PIECES]
    scores, mixed_rows, blocks, made, sems = refs[13 + 2 * PIECES :]
    scale = HD ** (-0.5)
    pool = given[5]
    sources = [*given[:5], pool.at[0], pool.at[1]]
    copies = [
        pltpu.make_async_copy(source, buf, sems.at[i])
        for i, (source, buf) in enumerate(zip(sources, held_in))
    ]
    for c in copies:
        c.start()
    pre, lens, table, dec, weight, keys, values = held_in
    copies[0].wait()
    spans, _, span, _ = pre.shape
    part = span // 2
    for r in range(spans):
        for h in range(2):
            width = part * (h + 1)
            q = pre[r, 0, h * part : (h + 1) * part, :]
            k = pre[r, 1, :width, :]
            v = pre[r, 2, :width, :]
            s = dot_nt(q, k) * scale
            row = lax.broadcasted_iota(jnp.int32, s.shape, 0) + h * part
            col = lax.broadcasted_iota(jnp.int32, s.shape, 1)
            s = jnp.where(col <= row, s, NEG_FILL)
            p = jnp.exp(s - jnp.max(s, axis=-1, keepdims=True))
            w = (p / jnp.sum(p, axis=-1, keepdims=True)).astype(BF)
            at = r * span + h * part
            mixed_rows[at : at + part, :] = dot(w, v).astype(BF).astype(F32)
    for c in copies[1:5]:
        c.wait()
    requests, entries = table.shape
    pages, page = keys.shape[0], keys.shape[1]
    square = (requests, requests)
    diagonal = lax.broadcasted_iota(jnp.int32, square, 0) == lax.broadcasted_iota(jnp.int32, square, 1)
    lengths = jnp.where(diagonal, jnp.broadcast_to(lens[...], square), 0).astype(F32)
    lengths = jnp.sum(lengths, axis=1, keepdims=True).astype(jnp.int32)
    held = jnp.clip(
        lengths - page * lax.broadcasted_iota(jnp.int32, (requests, entries), 1), 0, page
    )
    ids = table[...]
    lane = lax.broadcasted_iota(jnp.int32, (requests, page), 1)
    limit = jnp.zeros((requests, page), jnp.int32)
    for j in range(entries):
        limit = limit + jnp.where(ids[:, j : j + 1] == lane, held[:, j : j + 1], 0)
    q = dec[0]
    own = jnp.sum(q.astype(F32) * dec[1].astype(F32), axis=-1, keepdims=True) * scale
    group = 4
    wide = group * page
    copies[5].wait()
    top = jnp.full((requests, wide), NEG_FILL, F32)
    for c in range(pages // group):
        k = keys[c * group : (c + 1) * group].reshape(wide, HD)
        s = dot_nt(q, k) * scale
        s = jnp.concatenate(
            [
                jnp.where(
                    lane < limit[:, c * group + g : c * group + g + 1],
                    s[:, g * page : (g + 1) * page],
                    NEG_FILL,
                )
                for g in range(group)
            ],
            axis=1,
        )
        scores[:, c * wide : (c + 1) * wide] = s
        top = jnp.maximum(top, s)
    top = jnp.maximum(jnp.max(top, axis=-1, keepdims=True), own)
    total = jnp.zeros((requests, wide), F32)
    for c in range(pages // group):
        p = jnp.exp(scores[:, c * wide : (c + 1) * wide] - top)
        scores[:, c * wide : (c + 1) * wide] = p
        total = total + p
    own = jnp.exp(own - top)
    total = jnp.sum(total, axis=-1, keepdims=True) + own
    copies[6].wait()
    mixed = (own / total).astype(BF).astype(F32) * dec[2].astype(F32)
    for c in range(pages // group):
        w = (scores[:, c * wide : (c + 1) * wide] / total).astype(BF)
        mixed = mixed + dot(w, values[c * group : (c + 1) * group].reshape(wide, HD))
    mixed_rows[spans * span : spans * span + requests, :] = mixed.astype(BF).astype(F32)

    real = lax.broadcasted_iota(jnp.int32, (ROWS, HD), 0) < TOKENS
    for i in range(SIDE * SIDE):
        blocks[i] = jnp.where(real, mixed_rows[i * TOKENS : i * TOKENS + ROWS, :], 0.0)
    half = weight.shape[1] // 2
    at_x, at_z = mine[0] // SIDE, mine[0] % SIDE

    def rows(picked):
        return jnp.concatenate([blocks[i] for i in picked], axis=0).astype(BF)

    xs = [jnp.bitwise_xor(at_x, d) * SIDE for d in range(SIDE)]
    zs = [jnp.bitwise_xor(at_z, d) for d in range(SIDE)]
    middle = SIDE * ROWS // 2
    sent = []

    def send(at, place, out):
        sent.append(pltpu.make_async_copy(place, out, sems.at[at]))
        sent[-1].start()

    for d in (2, 1, 3, 0):
        for f, picked in enumerate(([xs[d] + z for z in zs], [x + zs[d] for x in xs])):
            i, first = f * SIDE + d, f * PIECES
            made[i] = dot(rows(picked), weight[:, f * half : (f + 1) * half]).astype(BF)
            at = len(copies) + first
            if d == 2:
                send(at + 3, made.at[i, pl.ds(0, middle)], outs[first + 3])
                send(at + 4, made.at[i, pl.ds(middle, middle)], outs[first + 4])
            else:
                place = {0: 0, 1: 1, 3: 2}[d]
                send(at + place, made.at[i], outs[first + place])
    for c in sent:
        c.wait()


def attention(mine, prefill_qkv, decode_qkv, cache_pool, page_table, cache_len, out_weight):
    requests = decode_qkv.shape[0]
    pages, page = cache_pool.shape[1:3]
    half = out_weight.shape[1] // 2
    given = [
        prefill_qkv,
        cache_len[None, :],
        page_table,
        decode_qkv.transpose(1, 0, 2),
        out_weight,
        cache_pool,
    ]
    return pl.pallas_call(
        attention_kernel,
        out_shape=part_shapes(half) * 2,
        in_specs=[pl.BlockSpec(memory_space=pltpu.SMEM)]
        + [pl.BlockSpec(memory_space=pltpu.HBM)] * len(given),
        out_specs=[pl.BlockSpec(memory_space=pltpu.HBM)] * (2 * PIECES),
        scratch_shapes=[pltpu.VMEM(a.shape, a.dtype) for a in given[:5]]
        + [
            pltpu.VMEM((pages, page, HD), BF),
            pltpu.VMEM((pages, page, HD), BF),
            pltpu.VMEM((requests, pages * page), F32),
            pltpu.VMEM((SIDE * SIDE * TOKENS + 8, HD), F32),
            pltpu.VMEM((SIDE * SIDE, ROWS, HD), F32),
            pltpu.VMEM((2 * SIDE, SIDE * ROWS, half), BF),
            pltpu.SemaphoreType.DMA((7 + 2 * PIECES,)),
        ],
        compiler_params=vmem(56),
        name="attention",
    )(mine, *given)


def along_x(a, d):
    return lax.ppermute(a, "exp", [(i, i ^ (d * SIDE)) for i in range(SIDE * SIDE)])


def along_z(a, d):
    return lax.ppermute(a, "exp", [(i, i ^ d) for i in range(SIDE * SIDE)])


def add_up(parts):
    total = parts[0].astype(F32)
    for p in parts[1:]:
        total = total + p.astype(F32)
    return total


def part_shapes(half):
    rows = SIDE * ROWS
    return [jax.ShapeDtypeStruct((n, half), BF) for n in (rows, rows, rows, rows // 2, rows // 2)]


def ring_sum(parts, along):
    half = parts[3].shape[0]
    near = along(parts[3], 1)
    far = along(parts[4], 3)
    one = jnp.concatenate([parts[1][:half], add_up([parts[1][half:], far]).astype(BF)], axis=0)
    three = jnp.concatenate([add_up([parts[2][:half], near]).astype(BF), parts[2][half:]], axis=0)
    return one, three


def sum_first(parts):
    parts_a, parts_b = parts[:PIECES], parts[PIECES:]
    one_a, three_a = ring_sum(parts_a, along_x)
    one_b, three_b = ring_sum(parts_b, along_z)
    one_a, three_a, one_b, three_b = lax.optimization_barrier((one_a, three_a, one_b, three_b))
    got_a = [parts_a[0], along_x(one_a, 1), along_x(three_a, 3)]
    got_b = [parts_b[0], along_z(one_b, 1), along_z(three_b, 3)]
    sum_a = add_up(got_a).astype(BF).reshape(SIDE, ROWS, -1)
    sum_b = add_up(got_b).astype(BF).reshape(SIDE, ROWS, -1)
    return sum_a, sum_b


def sum_second(sum_a, sum_b):
    got_a, got_b = [sum_a[0]], [sum_b[0]]
    for d in (1, 3, 2):
        got_a.append(along_z(sum_a[d], d))
        got_b.append(along_x(sum_b[d], d))
    return got_a, got_b


def gather(rows):
    half = rows.shape[1] // 2
    rows_a, rows_b = rows[:, :half], rows[:, half:]
    got_a, got_b = {0: rows_a}, {0: rows_b}
    for d in (1, 3, 2):
        got_a[d] = along_z(rows_a, d)
        got_b[d] = along_x(rows_b, d)
    rows_a = jnp.stack([got_a[d] for d in range(SIDE)])
    rows_b = jnp.stack([got_b[d] for d in range(SIDE)])
    rows_a, rows_b = lax.optimization_barrier((rows_a, rows_b))
    one_a, one_b = along_x(rows_a, 1), along_z(rows_b, 1)
    three_a, three_b = along_x(rows_a, 3), along_z(rows_b, 3)
    half = SIDE // 2
    return (
        [rows_a, one_a, three_a, along_x(three_a[:half], 1), along_x(one_a[half:], 3)],
        [rows_b, one_b, three_b, along_z(three_b[:half], 1), along_z(one_b[half:], 3)],
    )


def block_of(pieces, d, i):
    if d == 2:
        return pieces[3][i] if i < SIDE // 2 else pieces[4][i - SIDE // 2]
    return pieces[{0: 0, 1: 1, 3: 2}[d]][i]


def token_kernel(a0, a1, a2, a3, b0, b1, b2, b3, residual, gain, tags, stream, normed):
    f = lambda r: r[...].astype(F32)
    projected = jnp.concatenate(
        [f(a0) + f(a1) + f(a2) + f(a3), f(b0) + f(b1) + f(b2) + f(b3)], axis=1
    )
    held = (f(residual) + projected).astype(BF)
    stream[...] = held
    wide = held.astype(F32)
    mean = jnp.mean(wide * wide, axis=-1, keepdims=True)
    rows = wide * lax.rsqrt(mean + 1e-06) * gain[...]
    normed[...] = rows.astype(BF)
    count, lanes = tags.shape
    is_tag = lax.broadcasted_iota(jnp.int32, (count, lanes), 0) >= TOKENS
    normed[:, :lanes] = jnp.where(is_tag, tags[...], rows[:, :lanes]).astype(BF)


def chosen_rows(mine, rows_a, columns, capacity):
    shape = (columns, LANES)
    expert = lax.broadcasted_iota(jnp.int32, shape, 0) * (SIDE * SIDE // 2) + mine // 2
    expert = expert.astype(F32)
    hits = []
    for x in range(SIDE):
        for z in range(SIDE):
            tags = block_of(rows_a, x, z)[:, :LANES].astype(F32)
            hit = jnp.zeros(shape, F32)
            for k in range(ROUTES):
                named = jnp.broadcast_to(tags[TOKENS + k : TOKENS + k + 1, :], shape)
                hit = jnp.where(named == expert, 1.0, hit)
            hits.append(hit)
    hits = jnp.concatenate(hits, axis=0)
    before = lax.broadcasted_iota(jnp.int32, (LANES, LANES), 0) < lax.broadcasted_iota(
        jnp.int32, (LANES, LANES), 1
    )
    rank = dot(hits.astype(BF), before.astype(F32).astype(BF))
    rank = jnp.where(hits > 0.0, rank, -1.0)
    slot = lax.broadcasted_iota(jnp.int32, (columns, capacity, LANES), 1).astype(F32)
    chosen = []
    for i in range(SIDE * SIDE):
        here = rank[i * columns : (i + 1) * columns, :]
        here = jnp.broadcast_to(here[:, None, :], (columns, capacity, LANES))
        here = jnp.where(here == slot, 1.0, 0.0).reshape(columns * capacity, LANES)
        chosen.append(here[:, :ROWS].astype(BF))
    return chosen


def pick_kernel(mine, *refs):
    given, out, held = refs[: 2 * PIECES], refs[2 * PIECES], refs[2 * PIECES + 1 : 4 * PIECES + 1]
    made, in_sems, out_sems = refs[4 * PIECES + 1 :]
    columns, blocks, capacity, width = out.shape
    half = width // 2
    arriving = [
        pltpu.make_async_copy(source, place, in_sems.at[i])
        for i, (source, place) in enumerate(zip(given, held))
    ]
    for c in arriving:
        c.start()
    rows_a, rows_b = held[:PIECES], held[PIECES:]
    for c in arriving[:PIECES]:
        c.wait()
    chosen = chosen_rows(mine[0], rows_a, columns, capacity)
    for c in arriving[PIECES:]:
        c.wait()
    leaving = []
    for x in range(SIDE):
        for z in range(SIDE):
            d = x * SIDE + z
            pick = chosen[d]
            a = dot(pick, block_of(rows_a, x, z)).reshape(columns, capacity, half).astype(BF)
            b = dot(pick, block_of(rows_b, z, x)).reshape(columns, capacity, half).astype(BF)
            made[d, :, :, :half] = a
            made[d, :, :, half:] = b
            place = out.at[:, jnp.bitwise_xor(mine[0], d)]
            leaving.append(pltpu.make_async_copy(made.at[d], place, out_sems.at[d]))
            leaving[-1].start()
    for c in leaving:
        c.wait()


def pick(mine, rows_a, rows_b, columns, capacity):
    width = 2 * rows_a[0].shape[-1]
    blocks = SIDE * SIDE
    given = [*rows_a, *rows_b]
    return pl.pallas_call(
        pick_kernel,
        out_shape=jax.ShapeDtypeStruct((columns, blocks, capacity, width), BF),
        in_specs=[pl.BlockSpec(memory_space=pltpu.SMEM)]
        + [pl.BlockSpec(memory_space=pltpu.HBM)] * len(given),
        out_specs=pl.BlockSpec(memory_space=pltpu.HBM),
        scratch_shapes=[pltpu.VMEM(a.shape, BF) for a in given]
        + [
            pltpu.VMEM((blocks, columns, capacity, width), BF),
            pltpu.SemaphoreType.DMA((len(given),)),
            pltpu.SemaphoreType.DMA((blocks,)),
        ],
        compiler_params=vmem(56),
        name="pick",
    )(mine, *given)


def expert_kernel(rows, gate_up, down, out):
    x = rows[...]
    gate = dot_nt(x, gate_up[0, 0])
    up = dot_nt(x, gate_up[0, 1])
    hidden = (gate / (1.0 + jnp.exp(-gate)) * up).astype(BF)
    out[...] = dot(hidden, down[0]).astype(BF)


def experts(rows, gate_up, down):
    count, width = rows.shape
    step = 512
    return pl.pallas_call(
        expert_kernel,
        grid=(count // step,),
        out_shape=jax.ShapeDtypeStruct((count, width), BF),
        in_specs=[
            pl.BlockSpec((step, width), lambda i: (i, 0)),
            pl.BlockSpec(gate_up.shape, lambda i: (0, 0, 0, 0)),
            pl.BlockSpec(down.shape, lambda i: (0, 0, 0)),
        ],
        out_specs=pl.BlockSpec((step, width), lambda i: (i, 0)),
        compiler_params=vmem(56),
        cost_estimate=pl.CostEstimate(
            flops=6 * count * width * down.shape[1],
            bytes_accessed=2 * (2 * count * width + 3 * width * down.shape[1]),
            transcendentals=count * down.shape[1],
        ),
        name="experts",
    )(rows, gate_up, down)


def shared_kernel(*refs):
    rows_a, rows_b = refs[:PIECES], refs[PIECES : 2 * PIECES]
    gate_up, down = refs[2 * PIECES : 2 * PIECES + 2]
    outs, hidden = refs[2 * PIECES + 2 : -1], refs[-1]
    half = down.shape[1] // 2
    for x in range(SIDE):
        a, b = (
            jnp.concatenate(blocks, axis=0).astype(BF)
            for blocks in (
                [block_of(rows_a, x, z).astype(F32) for z in range(SIDE)],
                [block_of(rows_b, z, x).astype(F32) for z in range(SIDE)],
            )
        )
        gate = dot_nt(a, gate_up[0, :, :half]) + dot_nt(b, gate_up[0, :, half:])
        up = dot_nt(a, gate_up[1, :, :half]) + dot_nt(b, gate_up[1, :, half:])
        hidden[x] = (gate / (1.0 + jnp.exp(-gate)) * up).reshape(SIDE, ROWS, -1)
    middle = SIDE * ROWS // 2
    for d in range(SIDE):
        for f, part in enumerate((hidden[d], hidden[:, d])):
            part = part.reshape(SIDE * ROWS, -1).astype(BF)
            made = dot(part, down[:, f * half : (f + 1) * half]).astype(BF)
            if d == 2:
                outs[f * PIECES + 3][...] = made[:middle]
                outs[f * PIECES + 4][...] = made[middle:]
            else:
                outs[f * PIECES + {0: 0, 1: 1, 3: 2}[d]][...] = made


def shared_expert(rows_a, rows_b, gate_up, down):
    half = down.shape[1] // 2
    count, width = SIDE * SIDE * ROWS, down.shape[1]
    return pl.pallas_call(
        shared_kernel,
        out_shape=part_shapes(half) * 2,
        scratch_shapes=[pltpu.VMEM((SIDE, SIDE, ROWS, down.shape[0]), F32)],
        compiler_params=vmem(48),
        cost_estimate=pl.CostEstimate(
            flops=6 * count * width * down.shape[0],
            bytes_accessed=2 * (2 * count * width + 3 * width * down.shape[0]),
            transcendentals=count * down.shape[0],
        ),
        name="shared_expert",
    )(*rows_a, *rows_b, gate_up, down)


def on_device(
    residual,
    prefill_qkv,
    decode_qkv,
    cache_pool,
    page_table,
    cache_len,
    out_weight,
    norm_gain,
    shared_gate_up,
    shared_down,
    shared_gate,
    routes,
    route_weight,
    expert_gate_up,
    expert_down,
):
    mine = lax.axis_index("exp")
    groups = lax.axis_size("exp")
    tok_rows, width = residual.shape
    devices = groups * lax.axis_size("req")
    experts_all = devices // 2
    route_count = routes.shape[1]
    capacity = 8

    flat = routes.reshape(-1)
    place = jnp.arange(flat.shape[0], dtype=jnp.int32)
    same = (flat[:, None] == flat[None, :]) & (place[None, :] < place[:, None])
    rank = jnp.sum(same.astype(jnp.int32), axis=1)
    slot_of = (flat * capacity + rank).reshape(tok_rows, route_count)
    slot_of = jnp.pad(slot_of, ((0, ROWS - tok_rows), (0, 0)), constant_values=-1)
    weight = jnp.pad(route_weight, ((0, ROWS - tok_rows), (0, 0)))
    tags = jnp.pad(
        routes.T.astype(F32),
        ((tok_rows, ROWS - tok_rows - route_count), (0, LANES - tok_rows)),
        constant_values=-1.0,
    )
    columns = jnp.arange(devices * capacity, dtype=jnp.int32)
    columns = columns // (2 * capacity) * capacity + columns % capacity
    mix = jnp.sum(
        jnp.where(slot_of[:, :, None] == columns[None, None, :], weight[:, :, None], 0.0), axis=1
    )
    mix_high = mix.astype(BF)
    mix_low = (mix - mix_high.astype(F32)).astype(BF)
    mix = jnp.concatenate([mix_high, mix_low], axis=0)

    parts = attention(
        mine[None], prefill_qkv, decode_qkv, cache_pool, page_table, cache_len, out_weight
    )
    sums = sum_first(parts)
    got_a, got_b = sum_second(*lax.optimization_barrier(sums))
    stream, normed = pl.pallas_call(
        token_kernel,
        out_shape=[jax.ShapeDtypeStruct((ROWS, width), BF)] * 2,
        compiler_params=vmem(32),
        name="token_rows",
    )(
        *got_a,
        *got_b,
        jnp.pad(residual, ((0, ROWS - tok_rows), (0, 0))),
        norm_gain[None, :],
        tags,
    )
    rows_a, rows_b = gather(normed)
    outgoing = pick(mine[None], rows_a, rows_b, lax.axis_size("req"), capacity)
    arrived = lax.all_to_all(
        outgoing.reshape(lax.axis_size("req"), groups * capacity, width),
        "req",
        split_axis=0,
        concat_axis=0,
        tiled=True,
    )
    sums = sum_first(shared_expert(rows_a, rows_b, shared_gate_up.transpose(0, 2, 1), shared_down))
    got_a, got_b = sum_second(*lax.optimization_barrier(sums))
    arrived, got_a, got_b = lax.optimization_barrier((arrived, got_a, got_b))
    answer = experts(arrived.reshape(devices * capacity, width), expert_gate_up.transpose(0, 1, 3, 2), expert_down)
    returned = lax.all_to_all(
        answer.reshape(devices, capacity, width),
        ("req", "exp"),
        split_axis=0,
        concat_axis=0,
        tiled=True,
    )
    shared = jnp.concatenate([add_up(got_a), add_up(got_b)], axis=1)
    shared_scale = jax.nn.sigmoid(dot(normed, shared_gate))
    routed = dot(mix, returned.reshape(devices * capacity, width))
    routed = routed[:ROWS] + routed[ROWS:]
    result = stream.astype(F32) + routed + shared_scale[:, None] * shared
    return result[:tok_rows].astype(BF)


def solution(mesh):
    placed = (
        P(("req", "exp"), None),
        P("req", None, None, "exp"),
        P("req", None, "exp"),
        P(None, "req", None, "exp"),
        P("req", None),
        P("req"),
        P("exp", None),
        P(),
        P(None, None, "exp"),
        P("exp", None),
        P(),
        P(("req", "exp"), None),
        P(("req", "exp"), None),
        P(("req", "exp"), None, None, None),
        P(("req", "exp"), None, None),
    )
    return jax.shard_map(
        on_device, mesh=mesh, in_specs=placed, out_specs=P(("req", "exp"), None), check_vma=False
    )
```
